32 devices in a mesh: space: 8 (over z, x), col: 4 (over y, core).
Axes of the slice: x: 2, y: 2, z: 4, core: 2. Of those that a mesh axis runs over, the one named last changes fastest.
Arguments:
- blocks: bfloat16 [640, 24, 128, 128], P('space', 'col'), may hold values from -0.109375 to 0.109375
- basis_tiles: bfloat16 [640, 128, 128], P('space'), may hold values from -6 to 6
- weights: float32 [640, 128], P('space'), may hold values from 0.1 to 1
- neighbour_device: int32 [640, 24], P('space', 'col'), may hold values from 0 to 7, as said below
- neighbour_row: int32 [640, 24], P('space', 'col'), may hold values from 0 to 79
- counts: int32 [640], P('space'), may hold values from 12 to 24
- aggregate: int32 [640], P('space'), may hold values from 0 to 9
- pair_slot: int32 [640, 24], P('space', 'col'), may hold values from 0 to 3
Outputs:
- coarse: float32 [320, 128, 128], P(('space', 'col'))
The draws below stay inside these ranges and needn't reach their ends.
Inputs may be any that keep to these rules, and one draw needn't show every extreme that they name: `neighbour_device`: among the slots of one device's 80 rows that fall to one index of col, exactly 15 name another device; no other device is named more than 3 times there, and some other device exactly 3 times.
All inputs are finite; a program needn't handle non-finite values.
Results may differ from the reference program's by a relative error of at most 0.0045.
Values may be sent and summed in bfloat16 or wider, within the bound.
No kernel may reach another device: no remote copies, remote signals or barrier semaphores. Data moves between devices by JAX's collectives and lax.ppermute only.
A program may use at most 128 MiB of HBM per device.

```python
import math
import jax
import jax.numpy as jnp
from jax import lax

BS = 128
CB = 128
K = 24
KC = 4
CAP = 3
RB = 80
NCD = 10
REMOTE = 15
NB = 640
N_SPACE = 8
N_COL = 4


def draw_neighbour_device(key, part):
    slot_count = K // N_COL
    slot_total = RB * slot_count

    def draw_group(space_pos, col_pos):
        group_key = jax.random.fold_in(jax.random.fold_in(jax.random.fold_in(key, 7), space_pos), col_pos)
        key_pool, key_order = jax.random.split(group_key)
        others = (space_pos + 2 + jnp.arange((N_SPACE - 2) * CAP, dtype=jnp.int32) // CAP) % N_SPACE
        others = jax.random.permutation(key_pool, others)
        successor = jnp.full((CAP,), (space_pos + 1) % N_SPACE, jnp.int32)
        own_slots = jnp.full((slot_total - REMOTE,), space_pos, jnp.int32)
        peer_list = jnp.concatenate([successor, others[:REMOTE - CAP], own_slots])
        peer_list = jax.random.permutation(key_order, peer_list)
        return peer_list.reshape(RB, slot_count)
    space_range = jnp.arange(N_SPACE, dtype=jnp.int32)
    col_range = jnp.arange(N_COL, dtype=jnp.int32)
    grouped = jax.vmap(jax.vmap(draw_group, (None, 0)), (0, None))(space_range, col_range)
    return jnp.transpose(grouped, (0, 2, 1, 3)).reshape(N_SPACE * RB, K).astype(jnp.int32)


def set_ends(array, key, least, largest):
    longest = array.shape.index(max(array.shape))
    spots = []
    for shift in (0, 1):
        where = [jax.random.randint(jax.random.fold_in(key, axis), (), 0, length) for axis, length in enumerate(array.shape)]
        where[longest] = (where[longest] + shift) % array.shape[longest]
        spots.append(tuple(where))
    return array.at[spots[0]].set(least).at[spots[1]].set(largest)


def block_scale(key, dims, cuts, smallest, high):
    def one(axis_at, blocks):
        draws = jax.random.uniform(jax.random.fold_in(jax.random.fold_in(key, 6), axis_at), (blocks,), jnp.float32, smallest / len(cuts), high / len(cuts))
        return jnp.repeat(jnp.exp(draws), dims[axis_at] // blocks).reshape((-1,) + (1,) * (len(dims) - axis_at - 1))

    factor_of = one(*cuts[0])
    for cut in cuts[1:]:
        factor_of = factor_of * one(*cut)
    return factor_of


def noise(key, shape, width, most, shards=(), kind=jnp.bfloat16):
    loudness = block_scale(key, shape, shards, -0.22, 0.18) if shards else 1.0
    values = jax.random.normal(key, shape, jnp.float32) * width * loudness
    return jnp.minimum(jnp.maximum(values, -most), most).astype(kind)


def setup_inputs(seed: int = 0) -> dict:
    key_of = jax.random.split(jax.random.key(seed), 9)
    return {
        "blocks": noise(key_of[0], (NB, K, BS, BS), (BS * K) ** -0.5, 0.109375, ((0, 8), (1, 4))),
        "basis_tiles": noise(key_of[1], (NB, BS, CB), 1.0, 6.0, ((0, 8),)),
        "weights": jnp.clip(jnp.exp(math.log(1.0) - 2.3025851 * jax.random.uniform(key_of[2], (NB, BS), jnp.float32) ** block_scale(key_of[2], (NB, BS), ((0, 8),), -0.2, 0.2)), 0.1, 1.0),
        "neighbour_device": draw_neighbour_device(jax.random.fold_in(key_of[8], 71), 0),
        "neighbour_row": set_ends(jax.random.randint(key_of[4], (NB, K), 0, RB), jax.random.fold_in(key_of[4], 1), 0, RB - 1).astype(jnp.int32),
        "counts": set_ends(jax.random.randint(key_of[5], (NB,), K // 2, K + 1), jax.random.fold_in(key_of[5], 1), K // 2, K).astype(jnp.int32),
        "aggregate": set_ends(jax.random.randint(key_of[6], (NB,), 0, NCD), jax.random.fold_in(key_of[6], 1), 0, NCD - 1).astype(jnp.int32),
        "pair_slot": set_ends(jax.random.randint(key_of[7], (NB, K), 0, KC), jax.random.fold_in(key_of[7], 1), 0, KC - 1).astype(jnp.int32),
    }


def reference(blocks, basis_tiles, weights, neighbour_device, neighbour_row, counts, aggregate, pair_slot):
    neighbour_id = (neighbour_device * RB + neighbour_row).astype(jnp.int32)
    usable = jnp.arange(K, dtype=jnp.int32)[None, :] < counts[:, None]
    masked = jnp.where(usable[:, :, None, None], blocks, jnp.zeros((), blocks.dtype))
    masked_group = masked.reshape(N_SPACE, RB, K, BS, BS)
    id_group = neighbour_id.reshape(N_SPACE, RB, K)

    def smooth(pieces):
        block_group, neighbour_ids = pieces
        fetched = basis_tiles[neighbour_ids].astype(jnp.float32)
        return jnp.einsum("rkab,rkbc->rac", block_group.astype(jnp.float32), fetched)

    smoothed = lax.map(smooth, (masked_group, id_group)).reshape(N_SPACE * RB, BS, CB)
    prolong = (basis_tiles.astype(jnp.float32) - weights[:, :, None] * smoothed).astype(jnp.bfloat16)
    targets = (aggregate[:, None] * KC + pair_slot).astype(jnp.int32)

    def galerkin(pieces):
        block_group, neighbour_ids, own_tiles, target_group = pieces
        fetched = prolong[neighbour_ids].astype(jnp.float32)
        applied = jnp.einsum("rkab,rkbc->rkac", block_group.astype(jnp.float32), fetched).astype(jnp.bfloat16)
        contribution = jnp.einsum("rad,rkae->rkde", own_tiles.astype(jnp.float32), applied.astype(jnp.float32))
        return jax.ops.segment_sum(contribution.reshape(RB * K, CB, CB), target_group.reshape(RB * K), num_segments=NCD * KC)

    coarse = lax.map(galerkin, (masked_group, id_group, prolong.reshape(N_SPACE, RB, BS, CB), targets.reshape(N_SPACE, RB, K)))
    return coarse.reshape(N_SPACE * NCD * KC, CB, CB)
```

```python
import jax
import jax.numpy as jnp
from jax import lax
from jax.experimental import pallas as pl
from jax.experimental.pallas import tpu as pltpu
from jax.sharding import PartitionSpec as P

KC = 4
CAP = 3
NCD = 10
STATED_REMOTE = {8: 15, 32: 60}

F32 = jnp.float32
BF16 = jnp.bfloat16
VMEM_LIMIT = 56 * 1024 * 1024


def whole(shape):
    return pl.BlockSpec(shape, lambda *_: (0,) * len(shape))


def smem():
    return pl.BlockSpec(memory_space=pltpu.SMEM)


def hbm():
    return pl.BlockSpec(memory_space=pl.ANY)


def cost(flops, bytes_accessed):
    return pl.CostEstimate(flops=int(flops), bytes_accessed=int(bytes_accessed), transcendentals=0)


class Fields:
    def __init__(self, rows, targets, space):
        self.row_bits = max(1, (rows - 1).bit_length())
        self.target_bits = max(1, (targets - 1).bit_length())
        self.local_at = self.row_bits
        self.remote_at = self.row_bits + 1
        self.target_at = self.row_bits + 2
        self.device_at = self.target_at + self.target_bits

    def pack(self, row, local, remote, target, device):
        return (
            row
            + local.astype(jnp.int32) * (1 << self.local_at)
            + remote.astype(jnp.int32) * (1 << self.remote_at)
            + target * (1 << self.target_at)
            + device * (1 << self.device_at)
        )

    def row(self, code):
        return code & ((1 << self.row_bits) - 1)

    def local(self, code):
        return (code >> self.local_at) & 1

    def remote(self, code):
        return (code >> self.remote_at) & 1

    def target(self, code):
        return (code >> self.target_at) & ((1 << self.target_bits) - 1)

    def device(self, code):
        return code >> self.device_at


def list_remote(code, fields, rows, slots, space, most):
    def kernel(code_ref, ask_ref, row_ref, slot_ref, bucket_ref, target_ref, live_ref, used, count):
        for i in range(space * CAP):
            ask_ref[i] = 0
        for i in range(space):
            used[i] = 0
        count[0] = 0

        def clear(i, carry):
            row_ref[i] = 0
            slot_ref[i] = 0
            bucket_ref[i] = 0
            target_ref[i] = 0
            live_ref[i] = 0
            return carry

        lax.fori_loop(0, most, clear, 0)

        def one_row(r, carry):
            codes = [code_ref[r * slots + k] for k in range(slots)]
            seen = codes[0]
            for c in codes[1:]:
                seen = seen | c

            @pl.when(fields.remote(seen) == 1)
            def _():
                for k, c in enumerate(codes):

                    @pl.when(fields.remote(c) == 1)
                    def _():
                        device = fields.device(c)
                        place = device * CAP + used[device]
                        used[device] = used[device] + 1
                        ask_ref[place] = fields.row(c)
                        n = count[0]
                        row_ref[n] = r
                        slot_ref[n] = k
                        bucket_ref[n] = place
                        target_ref[n] = fields.target(c)
                        live_ref[n] = 1
                        count[0] = n + 1

            return carry

        lax.fori_loop(0, rows, one_row, 0)

    ints = lambda n: jax.ShapeDtypeStruct((n,), jnp.int32)
    return pl.pallas_call(
        kernel,
        out_shape=(ints(space * CAP),) + (ints(most),) * 5,
        in_specs=[smem()],
        out_specs=(smem(),) * 6,
        scratch_shapes=[pltpu.SMEM((space,), jnp.int32), pltpu.SMEM((1,), jnp.int32)],
        cost_estimate=cost(0, 1 << 20),
        name="list_remote",
    )(code)


def smooth_half(code, half, blocks, basis, added, fields, step):
    rows, slots, size, _ = blocks.shape
    coarse = basis.shape[2]
    steps = rows // 2 // step

    def kernel(code_ref, half_ref, blocks_ref, basis_ref, *rest):
        out_ref = rest[-1]
        first = (half_ref[0] * steps + pl.program_id(0)) * step
        for i in range(step):
            left, right = [], []
            for k in range(slots):
                c = code_ref[(first + i) * slots + k]
                tile = blocks_ref[i, k]
                left.append(jnp.where(fields.local(c) == 1, tile, jnp.zeros_like(tile)))
                right.append(basis_ref[fields.row(c)])
            total = jnp.dot(
                jnp.concatenate(left, axis=1), jnp.concatenate(right, axis=0), preferred_element_type=F32
            )
            if added is not None:
                total = total + rest[0][i].astype(F32)
            out_ref[i] = total.astype(BF16)

    operands = [blocks, basis] + ([] if added is None else [added])
    return pl.pallas_call(
        kernel,
        out_shape=jax.ShapeDtypeStruct((rows // 2, size, coarse), BF16),
        grid_spec=pltpu.PrefetchScalarGridSpec(
            num_scalar_prefetch=2,
            grid=(steps,),
            in_specs=[
                pl.BlockSpec((step, slots, size, size), lambda i, c, h: (h[0] * steps + i, 0, 0, 0)),
                pl.BlockSpec(basis.shape, lambda i, c, h: (0, 0, 0)),
            ]
            + ([] if added is None else [pl.BlockSpec((step, size, coarse), lambda i, c, h: (i, 0, 0))]),
            out_specs=pl.BlockSpec((step, size, coarse), lambda i, c, h: (i, 0, 0)),
        ),
        compiler_params=pltpu.CompilerParams(vmem_limit_bytes=VMEM_LIMIT),
        cost_estimate=cost(rows * slots * size * size * coarse, rows * slots * size * size),
        name="smooth_half",
    )(code, half, *operands)


def pick_tiles(index, tiles):
    count = index.shape[0]

    def kernel(index_ref, tiles_ref, out_ref, sem):
        def start(i, carry):
            pltpu.make_async_copy(tiles_ref.at[index_ref[i]], out_ref.at[i], sem).start()
            return carry

        lax.fori_loop(0, count, start, 0)
        pltpu.make_async_copy(out_ref, out_ref, sem).wait()

    return pl.pallas_call(
        kernel,
        out_shape=jax.ShapeDtypeStruct((count,) + tiles.shape[1:], tiles.dtype),
        in_specs=[smem(), hbm()],
        out_specs=hbm(),
        scratch_shapes=[pltpu.SemaphoreType.DMA],
        cost_estimate=cost(0, 2 * count * tiles.shape[1] * tiles.shape[2] * 2),
        name="pick_tiles",
    )(index, tiles)


def remote_sums(listing, blocks, received, weights):
    row, slot, bucket, _, live = listing
    most = row.shape[0]
    size, coarse = received.shape[1:]

    def kernel(row_ref, slot_ref, bucket_ref, live_ref, blocks_ref, received_ref, weights_ref, out_ref, tiles, sem):
        def start(j, carry):
            pltpu.make_async_copy(blocks_ref.at[row_ref[j], slot_ref[j]], tiles.at[j], sem).start()
            return carry

        lax.fori_loop(0, most, start, 0)
        pltpu.make_async_copy(tiles, tiles, sem).wait()

        def one(j, carry):
            total = jnp.dot(tiles[j], received_ref[bucket_ref[j]], preferred_element_type=F32)
            scale = jnp.transpose(jnp.broadcast_to(weights_ref[pl.ds(row_ref[j], 1), :], (8, size)))[:, :1]
            out_ref[j] = jnp.where(live_ref[j] == 1, total * scale, jnp.zeros_like(total)).astype(BF16)
            return carry

        lax.fori_loop(0, most, one, 0)

    return pl.pallas_call(
        kernel,
        out_shape=jax.ShapeDtypeStruct((most, size, coarse), BF16),
        in_specs=[smem()] * 4 + [hbm(), whole(received.shape), whole(weights.shape)],
        out_specs=whole((most, size, coarse)),
        grid=(1,),
        scratch_shapes=[pltpu.VMEM((most, size, size), BF16), pltpu.SemaphoreType.DMA],
        compiler_params=pltpu.CompilerParams(vmem_limit_bytes=VMEM_LIMIT),
        cost_estimate=cost(2 * most * size * size * coarse, 4 * most * size * size),
        name="remote_sums",
    )(row, slot, bucket, live, blocks, received, weights)


def local_prolong(half, basis, weights, own, other, step):
    rows, size, coarse = basis.shape
    steps = rows // 2 // step
    n = len(own)

    def kernel(half_ref, basis_ref, weights_ref, *rest):
        out_ref = rest[-1]

        def part(refs):
            scale = jnp.transpose(weights_ref[...])
            for i in range(step):
                total = refs[0][i].astype(F32)
                for ref in refs[1:]:
                    total = total + ref[i].astype(F32)
                out_ref[i] = basis_ref[i].astype(F32) - scale[:, i : i + 1] * total

        @pl.when(pl.program_id(0) == 0)
        def _():
            part(rest[:n])

        @pl.when(pl.program_id(0) == 1)
        def _():
            part(rest[n : 2 * n])

    at = lambda p, i, h: (jnp.where(p == 0, h[0], 1 - h[0]) * steps + i)
    return pl.pallas_call(
        kernel,
        out_shape=jax.ShapeDtypeStruct((rows, size, coarse), F32),
        grid_spec=pltpu.PrefetchScalarGridSpec(
            num_scalar_prefetch=1,
            grid=(2, steps),
            in_specs=[
                pl.BlockSpec((step, size, coarse), lambda p, i, h: (at(p, i, h), 0, 0)),
                pl.BlockSpec((step, size), lambda p, i, h: (at(p, i, h), 0)),
            ]
            + [pl.BlockSpec((step, size, coarse), lambda p, i, h: (jnp.where(p == 0, i, steps - 1), 0, 0))] * n
            + [pl.BlockSpec((step, size, coarse), lambda p, i, h: (jnp.where(p == 0, 0, i), 0, 0))] * n,
            out_specs=pl.BlockSpec((step, size, coarse), lambda p, i, h: (at(p, i, h), 0, 0)),
        ),
        compiler_params=pltpu.CompilerParams(vmem_limit_bytes=VMEM_LIMIT),
        cost_estimate=cost(0, rows * size * coarse * 10),
        name="local_prolong",
    )(half, basis, weights, *own, *other)


def finish_prolong(partial, sums, sum_rows, asked):
    rows, size, coarse = partial.shape
    n = len(sums)
    most = sums[0].shape[0]
    count = asked.shape[0]

    def kernel(asked_ref, *rest):
        row_refs, rest = rest[:n], rest[n:]
        partial_ref, sum_refs, out_ref, send_ref, work = rest[0], rest[1 : 1 + n], rest[1 + n], rest[2 + n], rest[3 + n]
        work[...] = partial_ref[...]
        for row_ref, sum_ref in zip(row_refs, sum_refs):

            def one(j, carry):
                r = row_ref[j]
                work[r] = work[r] - sum_ref[j].astype(F32)
                return carry

            lax.fori_loop(0, most, one, 0)

        def rounded(r, carry):
            out_ref[r] = work[r].astype(BF16)
            return carry

        lax.fori_loop(0, rows, rounded, 0)

        def send(i, carry):
            send_ref[i] = out_ref[asked_ref[i]]
            return carry

        lax.fori_loop(0, count, send, 0)

    return pl.pallas_call(
        kernel,
        out_shape=(
            jax.ShapeDtypeStruct((rows, size, coarse), BF16),
            jax.ShapeDtypeStruct((count, size, coarse), BF16),
        ),
        in_specs=[smem()] * (1 + n) + [whole(partial.shape)] + [whole(sums[0].shape)] * n,
        out_specs=(whole((rows, size, coarse)), whole((count, size, coarse))),
        grid=(1,),
        scratch_shapes=[pltpu.VMEM((rows, size, coarse), F32)],
        compiler_params=pltpu.CompilerParams(vmem_limit_bytes=VMEM_LIMIT),
        cost_estimate=cost(0, rows * size * coarse * 8),
        name="finish_prolong",
    )(asked, *sum_rows, partial, *sums)


def local_coarse(code, blocks, prolong, fields, targets, step):
    rows, slots, size, _ = blocks.shape
    coarse = prolong.shape[2]

    def kernel(code_ref, blocks_ref, prolong_ref, out_ref):
        first = pl.program_id(0) * step

        @pl.when(pl.program_id(0) == 0)
        def _():
            out_ref[...] = jnp.zeros_like(out_ref)

        for i in range(step):
            codes = [code_ref[(first + i) * slots + k] for k in range(slots)]
            applied = []
            for k, c in enumerate(codes):
                tile = blocks_ref[i, k]
                tile = jnp.where(fields.local(c) == 1, tile, jnp.zeros_like(tile))
                applied.append(
                    jnp.dot(tile, prolong_ref[fields.row(c)], preferred_element_type=F32).astype(BF16)
                )
            given = lax.dot_general(
                prolong_ref[first + i],
                jnp.concatenate(applied, axis=1),
                (((0,), (0,)), ((), ())),
                preferred_element_type=F32,
            )
            for k, c in enumerate(codes):
                out_ref[fields.target(c)] += given[:, k * coarse : (k + 1) * coarse]

    return pl.pallas_call(
        kernel,
        out_shape=jax.ShapeDtypeStruct((targets, coarse, coarse), F32),
        grid_spec=pltpu.PrefetchScalarGridSpec(
            num_scalar_prefetch=1,
            grid=(rows // step,),
            in_specs=[
                pl.BlockSpec((step, slots, size, size), lambda i, c: (i, 0, 0, 0)),
                pl.BlockSpec(prolong.shape, lambda i, c: (0, 0, 0)),
            ],
            out_specs=pl.BlockSpec((targets, coarse, coarse), lambda i, c: (0, 0, 0)),
        ),
        compiler_params=pltpu.CompilerParams(vmem_limit_bytes=VMEM_LIMIT),
        cost_estimate=cost(4 * rows * slots * size * size * coarse, 2 * rows * slots * size * size),
        name="local_coarse",
    )(code, blocks, prolong)


def remote_coarse(listing, core, blocks, prolong, received, local, chips):
    row, slot, bucket, target, live = listing
    most = row.shape[0]
    size, coarse = received.shape[1:]
    targets = local.shape[0]
    share = targets // (2 * chips)

    def kernel(
        core_ref, row_ref, slot_ref, bucket_ref, target_ref, live_ref,
        blocks_ref, prolong_ref, received_ref, local_ref, send_ref, keep_ref, tiles, own, sem,
    ):
        def start(j, carry):
            pltpu.make_async_copy(blocks_ref.at[row_ref[j], slot_ref[j]], tiles.at[j], sem.at[0]).start()
            pltpu.make_async_copy(prolong_ref.at[row_ref[j]], own.at[j], sem.at[1]).start()
            return carry

        lax.fori_loop(0, most, start, 0)
        for chip in range(chips):
            away = (2 * chip + 1 - core_ref[0]) * share
            here = (2 * chip + core_ref[0]) * share
            send_ref[chip] = local_ref[pl.ds(away, share)]
            keep_ref[chip] = local_ref[pl.ds(here, share)]
        pltpu.make_async_copy(tiles, tiles, sem.at[0]).wait()
        pltpu.make_async_copy(own, own, sem.at[1]).wait()

        def one(j, carry):
            applied = jnp.dot(tiles[j], received_ref[bucket_ref[j]], preferred_element_type=F32).astype(BF16)
            given = lax.dot_general(own[j], applied, (((0,), (0,)), ((), ())), preferred_element_type=F32)
            given = jnp.where(live_ref[j] == 1, given, jnp.zeros_like(given))
            owner = lax.div(target_ref[j], share)
            chip = lax.div(owner, 2)
            at = target_ref[j] - owner * share
            kept = (owner - 2 * chip) == core_ref[0]

            @pl.when(kept)
            def _():
                keep_ref[chip, at] += given

            @pl.when(jnp.logical_not(kept))
            def _():
                send_ref[chip, at] += given

            return carry

        lax.fori_loop(0, most, one, 0)

    out = jax.ShapeDtypeStruct((chips, share, coarse, coarse), F32)
    return pl.pallas_call(
        kernel,
        out_shape=(out, out),
        in_specs=[smem()] * 6 + [hbm(), hbm(), whole(received.shape), whole(local.shape)],
        out_specs=(whole(out.shape),) * 2,
        grid=(1,),
        scratch_shapes=[
            pltpu.VMEM((most, size, size), BF16),
            pltpu.VMEM((most, size, coarse), BF16),
            pltpu.SemaphoreType.DMA((2,)),
        ],
        compiler_params=pltpu.CompilerParams(vmem_limit_bytes=VMEM_LIMIT),
        cost_estimate=cost(4 * most * size * size * coarse, targets * coarse * coarse * 8),
        name="remote_coarse",
    )(core, row, slot, bucket, target, live, blocks, prolong, received, local)


def share_sums(chip, kept, arrived):
    chips, share, coarse, _ = kept.shape

    def kernel(chip_ref, kept_ref, arrived_ref, own_ref, *send_refs):
        for j in range(chips):
            at = chip_ref[0] + j
            at = jnp.where(at >= chips, at - chips, at)
            total = kept_ref[at] + arrived_ref[at]
            if j == 0:
                own_ref[...] = total
            else:
                send_refs[j - 1][...] = total.astype(BF16)

    tile = (share, coarse, coarse)
    return pl.pallas_call(
        kernel,
        out_shape=(jax.ShapeDtypeStruct(tile, F32),) + (jax.ShapeDtypeStruct(tile, BF16),) * (chips - 1),
        in_specs=[smem(), whole(kept.shape), whole(kept.shape)],
        out_specs=(whole(tile),) * chips,
        grid=(1,),
        compiler_params=pltpu.CompilerParams(vmem_limit_bytes=VMEM_LIMIT),
        cost_estimate=cost(0, kept.size * 12),
        name="share_sums",
    )(chip, kept, arrived)


def per_device(blocks, basis_tiles, weights, neighbour_device, neighbour_row, counts, aggregate, pair_slot):
    space = lax.axis_size("space")
    cols = lax.axis_size("col")
    chips = cols // 2
    own_index = lax.axis_index("space")
    col_index = lax.axis_index("col")
    rows, slots = neighbour_device.shape
    targets = NCD * KC
    most = min(STATED_REMOTE.get(space, CAP * (space - 1)), rows * slots)
    half_rows = rows // 2
    step = max(s for s in (1, 2, 4, 8) if half_rows % s == 0)
    fields = Fields(rows, targets, space)

    core = (col_index % 2).reshape(1).astype(jnp.int32)
    chip = (col_index // 2).reshape(1).astype(jnp.int32)

    def to_sibling(x):
        return lax.ppermute(x, "col", [(i, i ^ 1) for i in range(cols)])

    def to_chip(x, j):
        return lax.ppermute(x, "col", [(i, (i + 2 * j) % cols) for i in range(cols)])

    def to_owner(x):
        return lax.all_to_all(x, "space", split_axis=0, concat_axis=0, tiled=True)

    slot_number = col_index * slots + jnp.arange(slots, dtype=jnp.int32)
    live = slot_number[None, :] < counts[:, None]
    far = neighbour_device != own_index
    code = fields.pack(
        neighbour_row, live & ~far, live & far, aggregate[:, None] * KC + pair_slot, neighbour_device
    ).reshape(rows * slots)

    ask, *listing = list_remote(code, fields, rows, slots, space, most)
    asked = to_owner(ask.reshape(space, CAP)).reshape(space * CAP)

    sibling_sum = to_sibling(smooth_half(code, 1 - core, blocks, basis_tiles, None, fields, step))
    own_half = [smooth_half(code, core, blocks, basis_tiles, sibling_sum, fields, step)]
    own_half += [to_chip(own_half[0], j) for j in range(1, chips)]
    other_half = [to_sibling(x) for x in own_half]
    partial = local_prolong(core, basis_tiles, weights, own_half, other_half, step)

    received = to_owner(pick_tiles(asked, basis_tiles))
    own_sums = [(remote_sums(listing, blocks, received, weights), listing[0])]
    own_sums += [(to_chip(own_sums[0][0], j), to_chip(own_sums[0][1], j)) for j in range(1, chips)]
    sums = own_sums + [(to_sibling(x), to_sibling(r)) for x, r in own_sums]
    prolong, sent = finish_prolong(partial, [s for s, _ in sums], [r for _, r in sums], asked)

    received_prolong = to_owner(sent)
    coarse_local = local_coarse(code, blocks, prolong, fields, targets, step)
    send, keep = remote_coarse(listing, core, blocks, prolong, received_prolong, coarse_local, chips)
    own, *rest = share_sums(chip, keep, to_sibling(send))
    for j, part in enumerate(rest, 1):
        own = own + to_chip(part, j).astype(F32)
    return own


def solution(mesh):
    return jax.shard_map(
        per_device,
        mesh=mesh,
        in_specs=(
            P("space", "col", None, None),
            P("space", None, None),
            P("space", None),
            P("space", "col"),
            P("space", "col"),
            P("space"),
            P("space"),
            P("space", "col"),
        ),
        out_specs=P(("space", "col"), None, None),
        check_vma=False,
    )
```

```python
import jax
import jax.numpy as jnp
from jax import lax
from jax.experimental import pallas as pl
from jax.experimental.pallas import tpu as pltpu
from jax.sharding import PartitionSpec as P

KC = 4
CAP = 3
NCD = 10
STATED_REMOTE = {8: 15, 32: 60}

F32 = jnp.float32
BF16 = jnp.bfloat16
SMALL_VMEM = 6 << 20
LARGE_VMEM = 12 << 20
LANES = 128
ASK_ROWS = 8


def vmem():
    return pl.BlockSpec(memory_space=pltpu.VMEM)


def smem():
    return pl.BlockSpec(memory_space=pltpu.SMEM)


def for_each(n, body):
    if n <= 24:
        for j in range(n):
            body(j)
    else:
        lax.fori_loop(0, n, lambda j, carry: (body(j), carry)[1], 0, unroll=4)


def in_hbm(x):
    return pltpu.with_memory_space_constraint(x, pltpu.HBM)


def in_vmem(x):
    return pltpu.with_memory_space_constraint(x, pltpu.VMEM)


def hbm():
    return pl.BlockSpec(memory_space=pl.ANY)


def cost(flops, bytes_accessed):
    return pl.CostEstimate(flops=int(flops), bytes_accessed=int(bytes_accessed), transcendentals=0)


class Fields:
    def __init__(self, rows, targets, space):
        self.row_bits = max(1, (rows - 1).bit_length())
        self.target_bits = max(1, (targets - 1).bit_length())
        self.local_at = self.row_bits
        self.remote_at = self.row_bits + 1
        self.target_at = self.row_bits + 2
        self.device_at = self.target_at + self.target_bits

    def pack(self, row, local, remote, target, device):
        return (
            row
            + local.astype(jnp.int32) * (1 << self.local_at)
            + remote.astype(jnp.int32) * (1 << self.remote_at)
            + target * (1 << self.target_at)
            + device * (1 << self.device_at)
        )

    def row(self, code):
        return code & ((1 << self.row_bits) - 1)

    def local(self, code):
        return (code >> self.local_at) & 1

    def remote(self, code):
        return (code >> self.remote_at) & 1

    def target(self, code):
        return (code >> self.target_at) & ((1 << self.target_bits) - 1)

    def device(self, code):
        return code >> self.device_at


def list_remote(code, after, fields, rows, slots, space, most):
    def kernel(code_ref, after_ref, ask_ref, list_ref, used, count):
        del after_ref
        for i in range(space):
            used[i] = 0
            for j in range(CAP):
                ask_ref[i * ASK_ROWS, j] = 0
        count[0] = 0

        def clear(i, carry):
            list_ref[i] = 0
            return carry

        lax.fori_loop(0, Listing.FIELDS * most, clear, 0, unroll=5)

        def one_row(r, carry):
            codes = [code_ref[r * slots + k] for k in range(slots)]
            seen = codes[0]
            for c in codes[1:]:
                seen = seen | c

            @pl.when(fields.remote(seen) == 1)
            def _():
                for k, c in enumerate(codes):

                    @pl.when(fields.remote(c) == 1)
                    def _():
                        device = fields.device(c)
                        place = used[device]
                        used[device] = place + 1
                        ask_ref[device * ASK_ROWS, place] = fields.row(c)
                        n = count[0]
                        list_ref[n] = r
                        list_ref[most + n] = k
                        list_ref[2 * most + n] = device * CAP + place
                        list_ref[3 * most + n] = fields.target(c)
                        list_ref[4 * most + n] = 1
                        count[0] = n + 1

            return carry

        lax.fori_loop(0, rows, one_row, 0, unroll=2)

    return pl.pallas_call(
        kernel,
        out_shape=(
            jax.ShapeDtypeStruct((space * ASK_ROWS, LANES), jnp.int32),
            jax.ShapeDtypeStruct((Listing.FIELDS * most,), jnp.int32),
        ),
        in_specs=[smem(), hbm()],
        out_specs=(smem(), smem()),
        scratch_shapes=[pltpu.SMEM((space,), jnp.int32), pltpu.SMEM((1,), jnp.int32)],
        compiler_params=pltpu.CompilerParams(vmem_limit_bytes=SMALL_VMEM),
        cost_estimate=cost(0, 8 << 20),
        name="list_remote",
    )(code, after)


class Listing:
    FIELDS = 5

    def __init__(self, ref, most):
        self.row = lambda j: ref[j]
        self.slot = lambda j: ref[most + j]
        self.bucket = lambda j: ref[2 * most + j]
        self.target = lambda j: ref[3 * most + j]
        self.live = lambda j: ref[4 * most + j] == 1


def smooth_rows(first, rows, slots, step, code_ref, blocks_ref, basis_ref, fields, store):
    for i in range(step):
        r = rows + i
        left, right = [], []
        for k in range(slots):
            c = code_ref[(first + r) * slots + k]
            tile = blocks_ref[first + r, k]
            left.append(jnp.where(fields.local(c) == 1, tile, jnp.zeros_like(tile)))
            right.append(basis_ref[fields.row(c)])
        store(
            r,
            i,
            jnp.dot(jnp.concatenate(left, axis=1), jnp.concatenate(right, axis=0), preferred_element_type=F32),
        )


def smooth_first(code, half, blocks, basis, fields, step):
    rows, slots, size, _ = blocks.shape
    coarse = basis.shape[2]
    count = rows // 2
    steps = count // step

    def kernel(code_ref, half_ref, blocks_hbm, basis_hbm, out_ref, blocks_ref, basis_ref, block_sem, basis_sem):
        first = half_ref[0] * count
        rest = count - first
        load_basis = pltpu.make_async_copy(basis_hbm, basis_ref, basis_sem)
        load_basis.start()

        def load(j):
            at = pl.ds(first + j * step, step)
            return pltpu.make_async_copy(blocks_hbm.at[at], blocks_ref.at[at], block_sem.at[j])

        for j in range(steps):
            load(j).start()
        at = pl.ds(rest, count)
        load_rest = pltpu.make_async_copy(blocks_hbm.at[at], blocks_ref.at[at], block_sem.at[steps])
        load_rest.start()
        load_basis.wait()

        def one_step(j, carry):
            load(j).wait()

            def store(r, i, total):
                out_ref[r] = total.astype(BF16)

            smooth_rows(first, j * step, slots, step, code_ref, blocks_ref, basis_ref, fields, store)
            return carry

        lax.fori_loop(0, steps, one_step, 0)
        load_rest.wait()

    return pl.pallas_call(
        kernel,
        out_shape=(
            jax.ShapeDtypeStruct((count, size, coarse), BF16),
            pltpu.VMEM(blocks.shape, blocks.dtype),
            pltpu.VMEM(basis.shape, basis.dtype),
        ),
        in_specs=[smem(), smem(), hbm(), hbm()],
        out_specs=(vmem(), vmem(), vmem()),
        scratch_shapes=[pltpu.SemaphoreType.DMA((steps + 1,)), pltpu.SemaphoreType.DMA],
        compiler_params=pltpu.CompilerParams(vmem_limit_bytes=SMALL_VMEM),
        cost_estimate=cost(4 * rows * slots * size * size * coarse, rows * slots * size * size),
        name="smooth_first",
    )(code, half, in_hbm(blocks), in_hbm(basis))


def smooth_second(code, half, blocks, basis, weights, added, after, fields, step):
    rows, slots, size, _ = blocks.shape
    coarse = basis.shape[2]
    count = rows // 2

    def kernel(code_ref, half_ref, blocks_ref, basis_ref, weights_ref, added_ref, after_hbm, out_ref):
        del after_hbm
        first = half_ref[0] * count

        def one_step(j, carry):
            scale = jnp.transpose(weights_ref[pl.ds(pl.multiple_of(first + j * step, step), step), :])

            def store(r, i, total):
                out_ref[r] = (scale[:, i : i + 1] * (total + added_ref[r].astype(F32))).astype(BF16)

            smooth_rows(first, j * step, slots, step, code_ref, blocks_ref, basis_ref, fields, store)
            return carry

        lax.fori_loop(0, count // step, one_step, 0)

    return pl.pallas_call(
        kernel,
        out_shape=jax.ShapeDtypeStruct((count, size, coarse), BF16),
        in_specs=[smem(), smem(), vmem(), vmem(), vmem(), vmem(), hbm()],
        out_specs=vmem(),
        compiler_params=pltpu.CompilerParams(vmem_limit_bytes=SMALL_VMEM),
        cost_estimate=cost(4 * rows * slots * size * size * coarse, rows * slots * size * size),
        name="smooth_second",
    )(code, half, in_vmem(blocks), in_vmem(basis), weights, added, after)


def pick_remote_blocks(listing, blocks, after, most):
    def kernel(list_ref, blocks_hbm, after_hbm, out_ref, sem):
        del after_hbm
        entry = Listing(list_ref, most)

        def start(j):
            pltpu.make_async_copy(blocks_hbm.at[entry.row(j), entry.slot(j)], out_ref.at[j], sem).start()

        for_each(most, start)
        pltpu.make_async_copy(out_ref, out_ref, sem).wait()

    return pl.pallas_call(
        kernel,
        out_shape=pltpu.HBM((most,) + blocks.shape[2:], blocks.dtype),
        in_specs=[smem(), hbm(), hbm()],
        out_specs=vmem(),
        scratch_shapes=[pltpu.SemaphoreType.DMA],
        compiler_params=pltpu.CompilerParams(vmem_limit_bytes=SMALL_VMEM),
        cost_estimate=cost(0, 4 << 20),
        name="pick_remote_blocks",
    )(listing, in_hbm(blocks), after)


def pick_tiles(asked, tiles, space):
    count = space * CAP

    def kernel(asked_ref, tiles_ref, out_ref):
        for i in range(space):
            for j in range(CAP):
                out_ref[i * CAP + j] = tiles_ref[asked_ref[i * ASK_ROWS, j]]

    return pl.pallas_call(
        kernel,
        out_shape=pltpu.HBM((count,) + tiles.shape[1:], tiles.dtype),
        in_specs=[smem(), vmem()],
        out_specs=vmem(),
        compiler_params=pltpu.CompilerParams(vmem_limit_bytes=SMALL_VMEM),
        cost_estimate=cost(0, 4 << 20),
        name="pick_tiles",
    )(asked, in_vmem(tiles))


def remote_sums(listing, tiles, received, weights, after):
    most, size, _ = tiles.shape
    coarse = received.shape[2]

    def kernel(list_ref, tiles_ref, received_ref, weights_ref, *rest):
        out_ref, token_ref = rest[-2:]
        token_ref[0] = 0
        entry = Listing(list_ref, most)

        def one(j):
            total = jnp.dot(tiles_ref[j], received_ref[entry.bucket(j)], preferred_element_type=F32)
            scale = weights_ref[pl.ds(entry.row(j), 1), :]
            scale = jnp.where(entry.live(j), scale, jnp.zeros_like(scale))
            scale = jnp.transpose(jnp.broadcast_to(scale, (8, size)))[:, :1]
            out_ref[j] = (total * scale).astype(BF16)

        for_each(most, one)

    return pl.pallas_call(
        kernel,
        out_shape=(
            jax.ShapeDtypeStruct((most, size, coarse), BF16),
            jax.ShapeDtypeStruct((1,), jnp.int32),
        ),
        in_specs=[smem()] + [vmem()] * 3 + [smem()] * len(after),
        out_specs=(vmem(), smem()),
        compiler_params=pltpu.CompilerParams(vmem_limit_bytes=SMALL_VMEM),
        cost_estimate=cost(2 * most * size * size * coarse, 8 << 20),
        name="remote_sums",
    )(listing, tiles, received, weights, *after)


def local_prolong(half, basis, own, other, after):
    rows, size, coarse = basis.shape
    count = rows // 2
    n = len(own)

    def kernel(half_ref, after_ref, basis_ref, *rest):
        del after_ref
        out_ref = rest[-1]

        def part(base, refs):
            def one(r, carry):
                total = refs[0][r].astype(F32)
                for ref in refs[1:]:
                    total = total + ref[r].astype(F32)
                out_ref[base + r] = basis_ref[base + r].astype(F32) - total
                return carry

            lax.fori_loop(0, count, one, 0, unroll=4)

        part(half_ref[0] * count, rest[:n])
        part((1 - half_ref[0]) * count, rest[n : 2 * n])

    return pl.pallas_call(
        kernel,
        out_shape=pltpu.VMEM((rows, size, coarse), F32),
        in_specs=[smem(), smem()] + [vmem()] * (1 + 2 * n),
        out_specs=vmem(),
        compiler_params=pltpu.CompilerParams(vmem_limit_bytes=LARGE_VMEM),
        cost_estimate=cost(0, rows * size * coarse * 10),
        name="local_prolong",
    )(half, after, basis, *own, *other)


def finish_prolong(partial, sums, lists, asked, space):
    rows, size, coarse = partial.shape
    n = len(sums)
    most = sums[0].shape[0]
    count = space * CAP
    step = max(d for d in range(1, 17) if rows % d == 0)

    def kernel(asked_ref, *rest):
        list_refs, rest = rest[:n], rest[n:]
        sum_refs, rest = rest[1 : 1 + n], rest[1 + n :]
        work, prolong_hbm, send_ref, out_ref, sem = rest
        for list_ref, sum_ref in zip(list_refs, sum_refs):
            entry = Listing(list_ref, most)

            def take(j):
                r = entry.row(j)
                work[r] = work[r] - sum_ref[j].astype(F32)

            for_each(most, take)

        def rounded(g, carry):
            for i in range(step):
                out_ref[g * step + i] = work[g * step + i].astype(BF16)
            at = pl.ds(g * step, step)
            pltpu.make_async_copy(out_ref.at[at], prolong_hbm.at[at], sem).start()
            return carry

        lax.fori_loop(0, rows // step, rounded, 0)
        for i in range(space):
            for j in range(CAP):
                send_ref[i * CAP + j] = out_ref[asked_ref[i * ASK_ROWS, j]]
        pltpu.make_async_copy(out_ref, prolong_hbm, sem).wait()

    return pl.pallas_call(
        kernel,
        out_shape=(
            pltpu.VMEM((rows, size, coarse), F32),
            pltpu.HBM((rows, size, coarse), BF16),
            pltpu.HBM((count, size, coarse), BF16),
        ),
        in_specs=[smem()] * (1 + n) + [vmem()] * (1 + n),
        out_specs=(vmem(), hbm(), vmem()),
        scratch_shapes=[pltpu.VMEM((rows, size, coarse), BF16), pltpu.SemaphoreType.DMA],
        input_output_aliases={1 + n: 0},
        compiler_params=pltpu.CompilerParams(vmem_limit_bytes=LARGE_VMEM),
        cost_estimate=cost(0, rows * size * coarse * 8),
        name="finish_prolong",
    )(asked, *lists, in_vmem(partial), *sums)[1:]


def local_coarse(code, listing, blocks, prolong, fields, targets, step, most):
    rows, slots, size, _ = blocks.shape
    coarse = prolong.shape[2]
    half = targets // 2
    steps = rows // step

    def kernel(code_ref, list_ref, blocks_hbm, prolong_hbm, keep_ref, send_ref, tiles_ref, own_ref, *scratch):
        blocks_ref, prolong_ref, work, applied, sem, psem = scratch
        load_prolong = pltpu.make_async_copy(prolong_hbm, prolong_ref, psem)
        load_prolong.start()

        def load(j):
            at = pl.ds(j * step, step)
            return pltpu.make_async_copy(blocks_hbm.at[at], blocks_ref.at[at], sem.at[j])

        for j in range(steps):
            load(j).start()
        work[...] = jnp.zeros_like(work)
        load_prolong.wait()

        def one_step(j, carry):
            load(j).wait()
            for i in range(step):
                for k in range(slots):
                    c = code_ref[(j * step + i) * slots + k]
                    tile = blocks_ref[j * step + i, k]
                    tile = jnp.where(fields.local(c) == 1, tile, jnp.zeros_like(tile))
                    applied[i, :, k * coarse : (k + 1) * coarse] = jnp.dot(
                        tile, prolong_ref[fields.row(c)], preferred_element_type=F32
                    ).astype(BF16)
            for i in range(step):
                given = lax.dot_general(
                    prolong_ref[j * step + i], applied[i], (((0,), (0,)), ((), ())), preferred_element_type=F32
                )
                for k in range(slots):
                    c = code_ref[(j * step + i) * slots + k]
                    work[fields.target(c)] += given[:, k * coarse : (k + 1) * coarse]
            return carry

        lax.fori_loop(0, steps, one_step, 0)
        keep_ref[...] = work[pl.ds(0, half)]
        send_ref[...] = work[pl.ds(half, half)]
        entry = Listing(list_ref, most)

        def pick(j):
            tiles_ref[j] = blocks_ref[entry.row(j), entry.slot(j)]
            own_ref[j] = prolong_ref[entry.row(j)]

        for_each(most, pick)

    out = (half, coarse, coarse)
    return pl.pallas_call(
        kernel,
        out_shape=(
            pltpu.HBM(out, F32),
            pltpu.HBM(out, F32),
            pltpu.HBM((most, size, size), BF16),
            pltpu.HBM((most, size, coarse), BF16),
        ),
        in_specs=[smem(), smem(), hbm(), hbm()],
        out_specs=(vmem(),) * 4,
        scratch_shapes=[
            pltpu.VMEM(blocks.shape, BF16),
            pltpu.VMEM(prolong.shape, BF16),
            pltpu.VMEM((targets, coarse, coarse), F32),
            pltpu.VMEM((step, size, slots * coarse), BF16),
            pltpu.SemaphoreType.DMA((steps,)),
            pltpu.SemaphoreType.DMA,
        ],
        compiler_params=pltpu.CompilerParams(vmem_limit_bytes=36 << 20),
        cost_estimate=cost(8 * rows * slots * size * size * coarse, 2 * rows * slots * size * size),
        name="local_coarse",
    )(code, listing, in_hbm(blocks), in_hbm(prolong))


def remote_coarse(listing, tiles, own, received):
    most, size, coarse = own.shape

    def kernel(list_ref, tiles_hbm, own_hbm, received_ref, out_ref, applied, tiles_ref, own_ref, sem):
        load_tiles = pltpu.make_async_copy(tiles_hbm, tiles_ref, sem.at[0])
        load_own = pltpu.make_async_copy(own_hbm, own_ref, sem.at[1])
        load_tiles.start()
        load_own.start()
        entry = Listing(list_ref, most)

        def apply(j):
            applied[j] = jnp.dot(tiles_ref[j], received_ref[entry.bucket(j)], preferred_element_type=F32).astype(BF16)

        def give(j):
            given = lax.dot_general(own_ref[j], applied[j], (((0,), (0,)), ((), ())), preferred_element_type=F32)
            out_ref[j] = jnp.where(entry.live(j), given, jnp.zeros_like(given)).astype(BF16)

        load_tiles.wait()
        for_each(most, apply)
        load_own.wait()
        for_each(most, give)

    return pl.pallas_call(
        kernel,
        out_shape=jax.ShapeDtypeStruct((most, coarse, coarse), BF16),
        in_specs=[smem(), hbm(), hbm(), vmem()],
        out_specs=vmem(),
        scratch_shapes=[
            pltpu.VMEM((most, size, coarse), BF16),
            pltpu.VMEM((most, size, size), BF16),
            pltpu.VMEM((most, size, coarse), BF16),
            pltpu.SemaphoreType.DMA((2,)),
        ],
        compiler_params=pltpu.CompilerParams(vmem_limit_bytes=SMALL_VMEM),
        cost_estimate=cost(4 * most * size * size * coarse, 8 << 20),
        name="remote_coarse",
    )(listing, in_hbm(tiles), in_hbm(own), received)


def share_sums(chip, kept, arrived, listing, given, sibling_listing, sibling_given, chips):
    half, coarse, _ = kept.shape
    share = half // chips
    most = given.shape[0]

    def kernel(chip_ref, list_ref, sibling_ref, kept_ref, arrived_ref, given_ref, sibling_given_ref, *rest):
        own_ref, send_refs, work = rest[0], rest[1:-1], rest[-1]
        work[...] = kept_ref[...] + arrived_ref[...]
        own_entry, sibling_entry = Listing(list_ref, most), Listing(sibling_ref, most)

        def add_own(j):
            at = own_entry.target(j)

            @pl.when(at < half)
            def _():
                work[at] += given_ref[j].astype(F32)

        def add_sibling(j):
            at_sibling = sibling_entry.target(j)

            @pl.when(at_sibling >= half)
            def _():
                work[at_sibling - half] += sibling_given_ref[j].astype(F32)

        for_each(most, add_own)
        for_each(most, add_sibling)
        for j in range(chips):
            at = chip_ref[0] + j
            at = jnp.where(at >= chips, at - chips, at)
            total = work[pl.ds(at * share, share)]
            if j == 0:
                own_ref[...] = total
            else:
                send_refs[j - 1][...] = total.astype(BF16)

    tile = (share, coarse, coarse)
    return pl.pallas_call(
        kernel,
        out_shape=(jax.ShapeDtypeStruct(tile, F32),) + (jax.ShapeDtypeStruct(tile, BF16),) * (chips - 1),
        in_specs=[smem()] * 3 + [vmem()] * 4,
        out_specs=(vmem(),) * chips,
        scratch_shapes=[pltpu.VMEM(kept.shape, F32)],
        compiler_params=pltpu.CompilerParams(vmem_limit_bytes=SMALL_VMEM),
        cost_estimate=cost(0, kept.size * 12),
        name="share_sums",
    )(chip, listing, sibling_listing, kept, arrived, given, sibling_given)


def per_device(blocks, basis_tiles, weights, neighbour_device, neighbour_row, counts, aggregate, pair_slot):
    space = lax.axis_size("space")
    cols = lax.axis_size("col")
    chips = cols // 2
    own_index = lax.axis_index("space")
    col_index = lax.axis_index("col")
    rows, slots = neighbour_device.shape
    targets = NCD * KC
    share = targets // cols
    most = min(STATED_REMOTE.get(space, CAP * (space - 1)), rows * slots)
    half_rows = rows // 2
    step = max(s for s in (1, 2, 4, 8) if half_rows % s == 0)
    fields = Fields(rows, targets, space)

    core_index = col_index % 2
    core = core_index.reshape(1).astype(jnp.int32)
    chip = (col_index // 2).reshape(1).astype(jnp.int32)

    def to_sibling(x):
        return lax.ppermute(x, "col", [(i, i ^ 1) for i in range(cols)])

    def to_chip(x, j):
        return lax.ppermute(x, "col", [(i, (i + 2 * j) % cols) for i in range(cols)])

    def to_owner(x):
        return lax.all_to_all(x, "space", split_axis=0, concat_axis=0, tiled=True)

    slot_number = col_index * slots + jnp.arange(slots, dtype=jnp.int32)
    live = slot_number[None, :] < counts[:, None]
    far = neighbour_device != own_index
    target = aggregate[:, None] * KC + pair_slot
    owner = target // share
    target = (owner % 2 != core_index) * (targets // 2) + (owner // 2) * share + target % share
    code = fields.pack(neighbour_row, live & ~far, live & far, target, neighbour_device).reshape(rows * slots)

    sent_half, near_blocks, near_basis = smooth_first(code, 1 - core, blocks, basis_tiles, fields, step)
    ask, listing = list_remote(code, sent_half, fields, rows, slots, space, most)
    asked = to_owner(ask)
    sibling_sum = to_sibling(sent_half)
    own_half = [smooth_second(code, core, near_blocks, near_basis, weights, sibling_sum, ask, fields, step)]
    own_half += [to_chip(own_half[0], j) for j in range(1, chips)]
    other_half = [to_sibling(x) for x in own_half]

    picked = pick_tiles(asked, near_basis, space)
    received = to_owner(picked)
    remote_blocks = pick_remote_blocks(listing, blocks, picked, most)
    lists = [listing] + [to_chip(listing, j) for j in range(1, chips)]
    lists += [to_sibling(x) for x in lists]
    own_sums, token = remote_sums(listing, remote_blocks, received, weights, lists[1:])
    sums = [own_sums] + [to_chip(own_sums, j) for j in range(1, chips)]
    partial = local_prolong(core, basis_tiles, own_half, other_half, token)
    partial, *sums = lax.optimization_barrier((partial, *sums))
    sums += [to_sibling(x) for x in sums]
    prolong, sent = finish_prolong(partial, sums, lists, asked, space)

    received_prolong = to_owner(sent)
    keep, send, remote_blocks, own_tiles = local_coarse(
        code, listing, blocks, prolong, fields, targets, step, most
    )
    arrived = to_sibling(send)
    given = remote_coarse(listing, remote_blocks, own_tiles, received_prolong)
    own, *rest = share_sums(chip, keep, arrived, listing, given, lists[chips], to_sibling(given), chips)
    for j, part in enumerate(rest, 1):
        own = own + to_chip(part, j).astype(F32)
    return own


def solution(mesh):
    return jax.shard_map(
        per_device,
        mesh=mesh,
        in_specs=(
            P("space", "col", None, None),
            P("space", None, None),
            P("space", None),
            P("space", "col"),
            P("space", "col"),
            P("space"),
            P("space"),
            P("space", "col"),
        ),
        out_specs=P(("space", "col"), None, None),
        check_vma=False,
    )
```

```python
import jax
import jax.numpy as jnp
from jax import lax
from jax.experimental import pallas as pl
from jax.experimental.pallas import tpu as pltpu
from jax.sharding import PartitionSpec as P

KC = 4
CAP = 3
NCD = 10
STATED_REMOTE = {8: 15, 32: 60}

F32 = jnp.float32
BF16 = jnp.bfloat16
AHEAD = 3
SMALL_VMEM = 6 << 20
LARGE_VMEM = 12 << 20
LANES = 128
ASK_ROWS = 8


def vmem():
    return pl.BlockSpec(memory_space=pltpu.VMEM)


def smem():
    return pl.BlockSpec(memory_space=pltpu.SMEM)


def for_each(n, body):
    if n <= 24:
        for j in range(n):
            body(j)
    else:
        lax.fori_loop(0, n, lambda j, carry: (body(j), carry)[1], 0, unroll=4)


def in_hbm(x):
    return pltpu.with_memory_space_constraint(x, pltpu.HBM)


def in_vmem(x):
    return pltpu.with_memory_space_constraint(x, pltpu.VMEM)


def hbm():
    return pl.BlockSpec(memory_space=pl.ANY)


def cost(flops, bytes_accessed):
    return pl.CostEstimate(flops=int(flops), bytes_accessed=int(bytes_accessed), transcendentals=0)


class Fields:
    def __init__(self, rows, targets, space):
        self.row_bits = max(1, (rows - 1).bit_length())
        self.target_bits = max(1, (targets - 1).bit_length())
        self.local_at = self.row_bits
        self.remote_at = self.row_bits + 1
        self.target_at = self.row_bits + 2
        self.device_at = self.target_at + self.target_bits

    def pack(self, row, local, remote, target, device):
        return (
            row
            + local.astype(jnp.int32) * (1 << self.local_at)
            + remote.astype(jnp.int32) * (1 << self.remote_at)
            + target * (1 << self.target_at)
            + device * (1 << self.device_at)
        )

    def row(self, code):
        return code & ((1 << self.row_bits) - 1)

    def local(self, code):
        return (code >> self.local_at) & 1

    def remote(self, code):
        return (code >> self.remote_at) & 1

    def target(self, code):
        return (code >> self.target_at) & ((1 << self.target_bits) - 1)

    def device(self, code):
        return code >> self.device_at


def list_remote(code, own, after, fields, rows, slots, space, most):
    def kernel(code_ref, own_ref, after_ref, ask_ref, list_ref, used, count):
        del after_ref
        for i in range(space):
            used[i] = 0
            for j in range(CAP):
                ask_ref[i * ASK_ROWS, j] = 0
        count[0] = 0

        def clear(i, carry):
            list_ref[i] = 0
            return carry

        lax.fori_loop(0, Listing.FIELDS * most, clear, 0, unroll=5)

        def one_row(r, carry):
            codes = [code_ref[r * slots + k] for k in range(slots)]
            seen = codes[0]
            for c in codes[1:]:
                seen = seen | c

            @pl.when(fields.remote(seen) == 1)
            def _():
                for k, c in enumerate(codes):

                    @pl.when(fields.remote(c) == 1)
                    def _():
                        device = fields.device(c)
                        place = used[device]
                        used[device] = place + 1
                        ask_ref[device * ASK_ROWS, place] = fields.row(c)
                        n = count[0]
                        list_ref[n] = r
                        list_ref[most + n] = k
                        list_ref[2 * most + n] = device * CAP + place
                        list_ref[3 * most + n] = fields.target(c)
                        list_ref[4 * most + n] = 1
                        gap = own_ref[0] - device
                        gap = jnp.where(gap < 0, gap + space, gap)
                        list_ref[5 * most + n] = (gap - 1) * CAP + place
                        count[0] = n + 1

            return carry

        lax.fori_loop(0, rows, one_row, 0, unroll=2)

    return pl.pallas_call(
        kernel,
        out_shape=(
            jax.ShapeDtypeStruct((space * ASK_ROWS, LANES), jnp.int32),
            jax.ShapeDtypeStruct((Listing.FIELDS * most,), jnp.int32),
        ),
        in_specs=[smem(), smem(), hbm()],
        out_specs=(smem(), smem()),
        scratch_shapes=[pltpu.SMEM((space,), jnp.int32), pltpu.SMEM((1,), jnp.int32)],
        compiler_params=pltpu.CompilerParams(vmem_limit_bytes=SMALL_VMEM),
        cost_estimate=cost(0, 8 << 20),
        name="list_remote",
    )(code, own, after)


class Listing:
    FIELDS = 6

    def __init__(self, ref, most):
        self.row = lambda j: ref[j]
        self.slot = lambda j: ref[most + j]
        self.bucket = lambda j: ref[2 * most + j]
        self.target = lambda j: ref[3 * most + j]
        self.live = lambda j: ref[4 * most + j] == 1
        self.near_bucket = lambda j: ref[5 * most + j]


def smooth_rows(first, rows, slots, step, code_ref, blocks_ref, basis_ref, fields, store):
    for i in range(step):
        r = rows + i
        left, right = [], []
        for k in range(slots):
            c = code_ref[(first + r) * slots + k]
            tile = blocks_ref[first + r, k]
            left.append(jnp.where(fields.local(c) == 1, tile, jnp.zeros_like(tile)))
            right.append(basis_ref[fields.row(c)])
        store(
            r,
            i,
            jnp.dot(jnp.concatenate(left, axis=1), jnp.concatenate(right, axis=0), preferred_element_type=F32),
        )


def smooth_first(code, half, blocks, basis, fields, step):
    rows, slots, size, _ = blocks.shape
    coarse = basis.shape[2]
    count = rows // 2
    steps = count // step

    def kernel(code_ref, half_ref, blocks_hbm, basis_hbm, out_ref, blocks_ref, basis_ref, block_sem, basis_sem):
        first = half_ref[0] * count
        rest = count - first
        load_basis = pltpu.make_async_copy(basis_hbm, basis_ref, basis_sem)
        load_basis.start()

        def load(j):
            at = pl.ds(first + j * step, step)
            return pltpu.make_async_copy(blocks_hbm.at[at], blocks_ref.at[at], block_sem.at[j])

        at = pl.ds(rest, count)
        load_rest = pltpu.make_async_copy(blocks_hbm.at[at], blocks_ref.at[at], block_sem.at[steps])
        load(0).start()
        load_basis.wait()
        ahead = min(AHEAD, steps)
        for j in range(1, ahead):
            load(j).start()

        def one_step(j, carry):
            load(j).wait()

            @pl.when(j + ahead < steps)
            def _():
                load(j + ahead).start()

            @pl.when(j + ahead == steps)
            def _():
                load_rest.start()

            def store(r, i, total):
                out_ref[r] = total.astype(BF16)

            smooth_rows(first, j * step, slots, step, code_ref, blocks_ref, basis_ref, fields, store)
            return carry

        lax.fori_loop(0, steps, one_step, 0)
        load_rest.wait()

    return pl.pallas_call(
        kernel,
        out_shape=(
            jax.ShapeDtypeStruct((count, size, coarse), BF16),
            pltpu.VMEM(blocks.shape, blocks.dtype),
            pltpu.VMEM(basis.shape, basis.dtype),
        ),
        in_specs=[smem(), smem(), hbm(), hbm()],
        out_specs=(vmem(), vmem(), vmem()),
        scratch_shapes=[pltpu.SemaphoreType.DMA((steps + 1,)), pltpu.SemaphoreType.DMA],
        compiler_params=pltpu.CompilerParams(vmem_limit_bytes=SMALL_VMEM),
        cost_estimate=cost(4 * rows * slots * size * size * coarse, rows * slots * size * size),
        name="smooth_first",
    )(code, half, in_hbm(blocks), in_hbm(basis))


def smooth_second(code, half, blocks, basis, weights, added, fields, step):
    rows, slots, size, _ = blocks.shape
    coarse = basis.shape[2]
    count = rows // 2

    def kernel(code_ref, half_ref, blocks_ref, basis_ref, weights_ref, added_ref, out_ref):
        first = half_ref[0] * count

        def one_step(j, carry):
            scale = jnp.transpose(weights_ref[pl.ds(pl.multiple_of(first + j * step, step), step), :])

            def store(r, i, total):
                out_ref[r] = (scale[:, i : i + 1] * (total + added_ref[r].astype(F32))).astype(BF16)

            smooth_rows(first, j * step, slots, step, code_ref, blocks_ref, basis_ref, fields, store)
            return carry

        lax.fori_loop(0, count // step, one_step, 0)

    return pl.pallas_call(
        kernel,
        out_shape=jax.ShapeDtypeStruct((count, size, coarse), BF16),
        in_specs=[smem(), smem(), vmem(), vmem(), vmem(), vmem()],
        out_specs=vmem(),
        compiler_params=pltpu.CompilerParams(vmem_limit_bytes=SMALL_VMEM),
        cost_estimate=cost(4 * rows * slots * size * size * coarse, rows * slots * size * size),
        name="smooth_second",
    )(code, half, in_vmem(blocks), in_vmem(basis), weights, added)


def pick_tiles(asked, own, tiles, space):
    def kernel(asked_ref, own_ref, tiles_ref, *rest):
        out_hbm, sem = rest[: space - 1], rest[-1]
        for i in range(space - 1):
            device = own_ref[0] + i + 1
            device = jnp.where(device >= space, device - space, device)
            for j in range(CAP):
                row = asked_ref[device * ASK_ROWS, j]
                pltpu.make_async_copy(tiles_ref.at[row], out_hbm[i].at[j], sem.at[i]).start()
        for i in range(space - 1):
            pltpu.make_async_copy(tiles_ref.at[pl.ds(0, CAP)], out_hbm[i], sem.at[i]).wait()

    shape = (CAP,) + tiles.shape[1:]
    return pl.pallas_call(
        kernel,
        out_shape=(pltpu.HBM(shape, tiles.dtype),) * (space - 1),
        in_specs=[smem(), smem(), vmem()],
        out_specs=(hbm(),) * (space - 1),
        scratch_shapes=[pltpu.SemaphoreType.DMA((space - 1,))],
        compiler_params=pltpu.CompilerParams(vmem_limit_bytes=SMALL_VMEM),
        cost_estimate=cost(0, 1 << 16),
        name="pick_tiles",
    )(asked, own, in_vmem(tiles))


def pick_remote_blocks(listing, blocks, after):
    most = listing.shape[0] // Listing.FIELDS

    def kernel(list_ref, blocks_hbm, after_hbm, out_ref, sem):
        del after_hbm
        entry = Listing(list_ref, most)

        def start(j):
            pltpu.make_async_copy(blocks_hbm.at[entry.row(j), entry.slot(j)], out_ref.at[j], sem).start()

        for_each(most, start)
        pltpu.make_async_copy(out_ref, out_ref, sem).wait()

    return pl.pallas_call(
        kernel,
        out_shape=pltpu.VMEM((most,) + blocks.shape[2:], blocks.dtype),
        in_specs=[smem(), hbm(), hbm()],
        out_specs=vmem(),
        scratch_shapes=[pltpu.SemaphoreType.DMA],
        compiler_params=pltpu.CompilerParams(vmem_limit_bytes=SMALL_VMEM),
        cost_estimate=cost(0, 1 << 16),
        name="pick_remote_blocks",
    )(listing, in_hbm(blocks), after)


def remote_sums(listing, tiles, received, weights):
    n = len(received)
    most, size, _ = tiles.shape
    coarse = received[0].shape[2]

    def kernel(list_ref, weights_ref, tiles_ref, *rest):
        received_refs, (out_ref, arrived) = rest[:n], rest[-2:]
        entry = Listing(list_ref, most)
        for i in range(n):
            arrived[i * CAP : (i + 1) * CAP] = received_refs[i][...]

        def one(j):
            total = jnp.dot(tiles_ref[j], arrived[entry.near_bucket(j)], preferred_element_type=F32)
            scale = weights_ref[pl.ds(entry.row(j), 1), :]
            scale = jnp.where(entry.live(j), scale, jnp.zeros_like(scale))
            scale = jnp.transpose(jnp.broadcast_to(scale, (8, size)))[:, :1]
            out_ref[j] = (total * scale).astype(BF16)

        for_each(most, one)

    return pl.pallas_call(
        kernel,
        out_shape=jax.ShapeDtypeStruct((most, size, coarse), BF16),
        in_specs=[smem(), vmem(), vmem()] + [vmem()] * n,
        out_specs=vmem(),
        scratch_shapes=[pltpu.VMEM((n * CAP, size, coarse), BF16)],
        compiler_params=pltpu.CompilerParams(vmem_limit_bytes=LARGE_VMEM),
        cost_estimate=cost(0, 1 << 16),
        name="remote_sums",
    )(listing, weights, in_vmem(tiles), *received)


def take_off(work, list_refs, sum_refs, most):
    for list_ref, sum_ref in zip(list_refs, sum_refs):
        entry = Listing(list_ref, most)

        def take(j):
            r = entry.row(j)
            work[r] = work[r] - sum_ref[j].astype(F32)

        for_each(most, take)


def local_prolong(half, basis, own, other, sums, lists):
    rows, size, coarse = basis.shape
    count = rows // 2
    n, m = len(own), len(sums)
    most = sums[0].shape[0]

    def kernel(half_ref, *rest):
        list_refs, basis_ref, rest = rest[:m], rest[m], rest[m + 1 :]
        out_ref = rest[-1]

        def part(base, refs):
            def one(r, carry):
                total = refs[0][r].astype(F32)
                for ref in refs[1:]:
                    total = total + ref[r].astype(F32)
                out_ref[base + r] = basis_ref[base + r].astype(F32) - total
                return carry

            lax.fori_loop(0, count, one, 0, unroll=4)

        part(half_ref[0] * count, rest[:n])
        part((1 - half_ref[0]) * count, rest[n : 2 * n])
        take_off(out_ref, list_refs, rest[2 * n : 2 * n + m], most)

    return pl.pallas_call(
        kernel,
        out_shape=pltpu.VMEM((rows, size, coarse), F32),
        in_specs=[smem()] * (1 + m) + [vmem()] * (1 + 2 * n + m),
        out_specs=vmem(),
        compiler_params=pltpu.CompilerParams(vmem_limit_bytes=LARGE_VMEM),
        cost_estimate=cost(0, rows * size * coarse * 10),
        name="local_prolong",
    )(half, *lists, basis, *own, *other, *sums)


def finish_prolong(partial, sums, lists, asked, space):
    rows, size, coarse = partial.shape
    n = len(sums)
    most = sums[0].shape[0]
    count = space * CAP
    step = max(d for d in range(1, 17) if rows % d == 0)

    def kernel(asked_ref, *rest):
        list_refs, rest = rest[:n], rest[n:]
        sum_refs, rest = rest[1 : 1 + n], rest[1 + n :]
        work, prolong_hbm, send_ref, out_ref, sem = rest
        take_off(work, list_refs, sum_refs, most)

        def rounded(g, carry):
            for i in range(step):
                out_ref[g * step + i] = work[g * step + i].astype(BF16)
            at = pl.ds(g * step, step)
            pltpu.make_async_copy(out_ref.at[at], prolong_hbm.at[at], sem).start()
            return carry

        lax.fori_loop(0, rows // step, rounded, 0)
        for i in range(space):
            for j in range(CAP):
                send_ref[i * CAP + j] = out_ref[asked_ref[i * ASK_ROWS, j]]
        pltpu.make_async_copy(out_ref, prolong_hbm, sem).wait()

    return pl.pallas_call(
        kernel,
        out_shape=(
            pltpu.VMEM((rows, size, coarse), F32),
            pltpu.HBM((rows, size, coarse), BF16),
            pltpu.HBM((count, size, coarse), BF16),
        ),
        in_specs=[smem()] * (1 + n) + [vmem()] * (1 + n),
        out_specs=(vmem(), hbm(), vmem()),
        scratch_shapes=[pltpu.VMEM((rows, size, coarse), BF16), pltpu.SemaphoreType.DMA],
        input_output_aliases={1 + n: 0},
        compiler_params=pltpu.CompilerParams(vmem_limit_bytes=LARGE_VMEM),
        cost_estimate=cost(0, rows * size * coarse * 8),
        name="finish_prolong",
    )(asked, *lists, in_vmem(partial), *sums)[1:]


def local_coarse(code, listing, blocks, prolong, fields, targets, step, most):
    rows, slots, size, _ = blocks.shape
    coarse = prolong.shape[2]
    half = targets // 2
    steps = rows // step

    def kernel(code_ref, list_ref, blocks_hbm, prolong_hbm, keep_ref, send_ref, tiles_ref, own_ref, *scratch):
        blocks_ref, prolong_ref, work, applied, sem, psem = scratch
        load_prolong = pltpu.make_async_copy(prolong_hbm, prolong_ref, psem)
        load_prolong.start()

        def load(j):
            at = pl.ds(j * step, step)
            return pltpu.make_async_copy(blocks_hbm.at[at], blocks_ref.at[at], sem.at[j])

        load(0).start()
        work[...] = jnp.zeros_like(work)
        load_prolong.wait()
        for j in range(1, min(AHEAD, steps)):
            load(j).start()

        def one_step(j, carry):
            load(j).wait()

            @pl.when(j + AHEAD < steps)
            def _():
                load(j + AHEAD).start()

            for i in range(step):
                for k in range(slots):
                    c = code_ref[(j * step + i) * slots + k]
                    tile = blocks_ref[j * step + i, k]
                    tile = jnp.where(fields.local(c) == 1, tile, jnp.zeros_like(tile))
                    applied[i, :, k * coarse : (k + 1) * coarse] = jnp.dot(
                        tile, prolong_ref[fields.row(c)], preferred_element_type=F32
                    ).astype(BF16)
            for i in range(step):
                given = lax.dot_general(
                    prolong_ref[j * step + i], applied[i], (((0,), (0,)), ((), ())), preferred_element_type=F32
                )
                for k in range(slots):
                    c = code_ref[(j * step + i) * slots + k]
                    work[fields.target(c)] += given[:, k * coarse : (k + 1) * coarse]
            return carry

        lax.fori_loop(0, steps, one_step, 0)
        keep_ref[...] = work[pl.ds(0, half)]
        send_ref[...] = work[pl.ds(half, half)]
        entry = Listing(list_ref, most)

        def pick(j):
            tiles_ref[j] = blocks_ref[entry.row(j), entry.slot(j)]
            own_ref[j] = prolong_ref[entry.row(j)]

        for_each(most, pick)

    out = (half, coarse, coarse)
    return pl.pallas_call(
        kernel,
        out_shape=(
            pltpu.HBM(out, F32),
            pltpu.HBM(out, F32),
            pltpu.HBM((most, size, size), BF16),
            pltpu.HBM((most, size, coarse), BF16),
        ),
        in_specs=[smem(), smem(), hbm(), hbm()],
        out_specs=(vmem(),) * 4,
        scratch_shapes=[
            pltpu.VMEM(blocks.shape, BF16),
            pltpu.VMEM(prolong.shape, BF16),
            pltpu.VMEM((targets, coarse, coarse), F32),
            pltpu.VMEM((step, size, slots * coarse), BF16),
            pltpu.SemaphoreType.DMA((steps,)),
            pltpu.SemaphoreType.DMA,
        ],
        compiler_params=pltpu.CompilerParams(vmem_limit_bytes=36 << 20),
        cost_estimate=cost(8 * rows * slots * size * size * coarse, 2 * rows * slots * size * size),
        name="local_coarse",
    )(code, listing, in_hbm(blocks), in_hbm(prolong))


def remote_coarse(listing, tiles, own, received):
    most, size, coarse = own.shape

    def kernel(list_ref, tiles_hbm, own_hbm, received_ref, out_ref, applied, tiles_ref, own_ref, sem):
        load_tiles = pltpu.make_async_copy(tiles_hbm, tiles_ref, sem.at[0])
        load_own = pltpu.make_async_copy(own_hbm, own_ref, sem.at[1])
        load_tiles.start()
        load_own.start()
        entry = Listing(list_ref, most)

        def apply(j):
            applied[j] = jnp.dot(tiles_ref[j], received_ref[entry.bucket(j)], preferred_element_type=F32).astype(BF16)

        def give(j):
            given = lax.dot_general(own_ref[j], applied[j], (((0,), (0,)), ((), ())), preferred_element_type=F32)
            out_ref[j] = jnp.where(entry.live(j), given, jnp.zeros_like(given)).astype(BF16)

        load_tiles.wait()
        for_each(most, apply)
        load_own.wait()
        for_each(most, give)

    return pl.pallas_call(
        kernel,
        out_shape=jax.ShapeDtypeStruct((most, coarse, coarse), BF16),
        in_specs=[smem(), hbm(), hbm(), vmem()],
        out_specs=vmem(),
        scratch_shapes=[
            pltpu.VMEM((most, size, coarse), BF16),
            pltpu.VMEM((most, size, size), BF16),
            pltpu.VMEM((most, size, coarse), BF16),
            pltpu.SemaphoreType.DMA((2,)),
        ],
        compiler_params=pltpu.CompilerParams(vmem_limit_bytes=SMALL_VMEM),
        cost_estimate=cost(4 * most * size * size * coarse, 8 << 20),
        name="remote_coarse",
    )(listing, in_hbm(tiles), in_hbm(own), received)


def share_sums(chip, kept, arrived, listing, given, sibling_listing, sibling_given, chips):
    half, coarse, _ = kept.shape
    share = half // chips
    most = given.shape[0]

    def kernel(chip_ref, list_ref, sibling_ref, kept_ref, arrived_ref, given_ref, sibling_given_ref, *rest):
        own_ref, send_refs, work = rest[0], rest[1:-1], rest[-1]
        work[...] = kept_ref[...] + arrived_ref[...]
        own_entry, sibling_entry = Listing(list_ref, most), Listing(sibling_ref, most)

        def add_own(j):
            at = own_entry.target(j)

            @pl.when(at < half)
            def _():
                work[at] += given_ref[j].astype(F32)

        def add_sibling(j):
            at_sibling = sibling_entry.target(j)

            @pl.when(at_sibling >= half)
            def _():
                work[at_sibling - half] += sibling_given_ref[j].astype(F32)

        for_each(most, add_own)
        for_each(most, add_sibling)
        for j in range(chips):
            at = chip_ref[0] + j
            at = jnp.where(at >= chips, at - chips, at)
            total = work[pl.ds(at * share, share)]
            if j == 0:
                own_ref[...] = total
            else:
                send_refs[j - 1][...] = total.astype(BF16)

    tile = (share, coarse, coarse)
    return pl.pallas_call(
        kernel,
        out_shape=(jax.ShapeDtypeStruct(tile, F32),) + (jax.ShapeDtypeStruct(tile, BF16),) * (chips - 1),
        in_specs=[smem()] * 3 + [vmem()] * 4,
        out_specs=(vmem(),) * chips,
        scratch_shapes=[pltpu.VMEM(kept.shape, F32)],
        compiler_params=pltpu.CompilerParams(vmem_limit_bytes=SMALL_VMEM),
        cost_estimate=cost(0, kept.size * 12),
        name="share_sums",
    )(chip, listing, sibling_listing, kept, arrived, given, sibling_given)


def per_device(blocks, basis_tiles, weights, neighbour_device, neighbour_row, counts, aggregate, pair_slot):
    space = lax.axis_size("space")
    cols = lax.axis_size("col")
    chips = cols // 2
    own_index = lax.axis_index("space")
    col_index = lax.axis_index("col")
    rows, slots = neighbour_device.shape
    targets = NCD * KC
    share = targets // cols
    most = min(STATED_REMOTE.get(space, CAP * (space - 1)), rows * slots)
    half_rows = rows // 2
    step = max(s for s in (1, 2, 4, 8) if half_rows % s == 0)
    fields = Fields(rows, targets, space)

    core_index = col_index % 2
    core = core_index.reshape(1).astype(jnp.int32)
    chip = (col_index // 2).reshape(1).astype(jnp.int32)
    own = own_index.reshape(1).astype(jnp.int32)

    def to_sibling(x):
        return lax.ppermute(x, "col", [(i, i ^ 1) for i in range(cols)])

    def to_chip(x, j):
        return lax.ppermute(x, "col", [(i, (i + 2 * j) % cols) for i in range(cols)])

    def to_distance(x, j):
        return lax.ppermute(x, "space", [(i, (i + j) % space) for i in range(space)])

    def to_owner(x):
        return lax.all_to_all(x, "space", split_axis=0, concat_axis=0, tiled=True)

    slot_number = col_index * slots + jnp.arange(slots, dtype=jnp.int32)
    live = slot_number[None, :] < counts[:, None]
    far = neighbour_device != own_index
    target = aggregate[:, None] * KC + pair_slot
    owner = target // share
    target = (owner % 2 != core_index) * (targets // 2) + (owner // 2) * share + target % share
    code = fields.pack(neighbour_row, live & ~far, live & far, target, neighbour_device).reshape(rows * slots)

    sent_half, near_blocks, near_basis = smooth_first(code, 1 - core, blocks, basis_tiles, fields, step)
    ask, listing = list_remote(code, own, sent_half, fields, rows, slots, space, most)
    lists = [listing] + [to_chip(listing, j) for j in range(1, chips)]
    sibling_sum, ask = lax.optimization_barrier((to_sibling(sent_half), ask))
    kept_half = smooth_second(code, core, near_blocks, near_basis, weights, sibling_sum, fields, step)
    kept_half, *lists = lax.optimization_barrier((kept_half, *lists))
    far_half = [to_chip(kept_half, j) for j in range(1, chips)]

    asked, sibling_lists = lax.optimization_barrier((to_owner(ask), [to_sibling(x) for x in lists]))
    picked = pick_tiles(asked, own, near_basis, space)
    received = [to_distance(x, j) for j, x in enumerate(picked, 1)]
    remote_blocks = pick_remote_blocks(listing, blocks, received[len(received) // 2])
    far_half, received, remote_blocks = lax.optimization_barrier((far_half, received, remote_blocks))
    own_half = [kept_half] + far_half
    other_half = [to_sibling(x) for x in own_half]
    own_sums = remote_sums(listing, remote_blocks, received, weights)
    far_sums = [to_chip(own_sums, j) for j in range(1, chips)]
    near_sums = [own_sums, to_sibling(own_sums)]
    partial = local_prolong(core, basis_tiles, own_half, other_half, near_sums, [listing, sibling_lists[0]])
    partial, *far_sums = lax.optimization_barrier((partial, *far_sums))
    far_sums += [to_sibling(x) for x in far_sums]
    prolong, sent = finish_prolong(partial, far_sums, lists[1:] + sibling_lists[1:], asked, space)

    received_prolong = to_owner(sent)
    keep, send, remote_blocks, own_tiles = local_coarse(
        code, listing, blocks, prolong, fields, targets, step, most
    )
    arrived = to_sibling(send)
    given = remote_coarse(listing, remote_blocks, own_tiles, received_prolong)
    total, *rest = share_sums(chip, keep, arrived, listing, given, sibling_lists[0], to_sibling(given), chips)
    for j, part in enumerate(rest, 1):
        total = total + to_chip(part, j).astype(F32)
    return total


def solution(mesh):
    return jax.shard_map(
        per_device,
        mesh=mesh,
        in_specs=(
            P("space", "col", None, None),
            P("space", None, None),
            P("space", None),
            P("space", "col"),
            P("space", "col"),
            P("space"),
            P("space"),
            P("space", "col"),
        ),
        out_specs=P(("space", "col"), None, None),
        check_vma=False,
    )
```

```python
import jax
import jax.numpy as jnp
from jax import lax
from jax.experimental import pallas as pl
from jax.experimental.pallas import tpu as pltpu
from jax.sharding import PartitionSpec as P

KC = 4
CAP = 3
NCD = 10
STATED_REMOTE = {8: 15, 32: 60}

F32 = jnp.float32
BF16 = jnp.bfloat16
AHEAD = 3
IN_FLIGHT = 4
SMALL_VMEM = 6 << 20
LARGE_VMEM = 12 << 20
LANES = 128
ASK_ROWS = 8


def vmem():
    return pl.BlockSpec(memory_space=pltpu.VMEM)


def smem():
    return pl.BlockSpec(memory_space=pltpu.SMEM)


def for_each(n, body):
    if n <= 24:
        for j in range(n):
            body(j)
    else:
        lax.fori_loop(0, n, lambda j, carry: (body(j), carry)[1], 0, unroll=4)


def in_hbm(x):
    return pltpu.with_memory_space_constraint(x, pltpu.HBM)


def in_vmem(x):
    return pltpu.with_memory_space_constraint(x, pltpu.VMEM)


def hbm():
    return pl.BlockSpec(memory_space=pl.ANY)


def cost(flops, bytes_accessed):
    return pl.CostEstimate(flops=int(flops), bytes_accessed=int(bytes_accessed), transcendentals=0)


class Fields:
    def __init__(self, rows):
        self.row_bits = max(1, (rows - 1).bit_length())
        self.local_at = self.row_bits
        self.remote_at = self.row_bits + 1
        self.device_at = self.row_bits + 2

    def pack(self, row, local, remote, device):
        return (
            row
            + local.astype(jnp.int32) * (1 << self.local_at)
            + remote.astype(jnp.int32) * (1 << self.remote_at)
            + device * (1 << self.device_at)
        )

    def row(self, code):
        return code & ((1 << self.row_bits) - 1)

    def local(self, code):
        return (code >> self.local_at) & 1

    def remote(self, code):
        return (code >> self.remote_at) & 1

    def device(self, code):
        return code >> self.device_at


def list_remote(code, own, after, fields, rows, slots, space, most):
    def kernel(code_ref, own_ref, after_ref, ask_ref, list_ref, used, found):
        del after_ref
        for i in range(space):
            used[i] = 0
            for j in range(CAP):
                ask_ref[i * ASK_ROWS, j] = 0

        def clear(i, carry):
            list_ref[i] = 0
            return carry

        lax.fori_loop(0, Listing.FIELDS * most, clear, 0, unroll=10)

        def look(r, count):
            for k in range(slots):
                found[count] = r * slots + k
                count = count + fields.remote(code_ref[r * slots + k])
            return count

        count = lax.fori_loop(0, rows, look, jnp.int32(0), unroll=8)

        def enter(n, carry):
            at = found[n]
            c = code_ref[at]
            row = lax.div(at, slots)
            device = fields.device(c)
            place = used[device]
            used[device] = place + 1
            ask_ref[device * ASK_ROWS, place] = fields.row(c)
            gap = own_ref[0] - device
            gap = jnp.where(gap < 0, gap + space, gap)
            list_ref[n] = row
            list_ref[most + n] = at - row * slots
            list_ref[2 * most + n] = device * CAP + place
            list_ref[3 * most + n] = at
            list_ref[4 * most + n] = 1
            list_ref[5 * most + n] = (gap - 1) * CAP + place
            return carry

        lax.fori_loop(0, count, enter, 0)

    return pl.pallas_call(
        kernel,
        out_shape=(
            jax.ShapeDtypeStruct((space * ASK_ROWS, LANES), jnp.int32),
            jax.ShapeDtypeStruct((Listing.FIELDS * most,), jnp.int32),
        ),
        in_specs=[smem(), smem(), hbm()],
        out_specs=(smem(), smem()),
        scratch_shapes=[pltpu.SMEM((space,), jnp.int32), pltpu.SMEM((rows * slots + 1,), jnp.int32)],
        compiler_params=pltpu.CompilerParams(vmem_limit_bytes=SMALL_VMEM),
        cost_estimate=cost(0, 8 << 20),
        name="list_remote",
    )(code, own, after)


class Listing:
    FIELDS = 6

    def __init__(self, ref, most):
        self.row = lambda j: ref[j]
        self.slot = lambda j: ref[most + j]
        self.bucket = lambda j: ref[2 * most + j]
        self.place = lambda j: ref[3 * most + j]
        self.live = lambda j: ref[4 * most + j] == 1
        self.near_bucket = lambda j: ref[5 * most + j]


def smooth_rows(first, rows, slots, step, code_ref, blocks_ref, basis_ref, fields, store):
    for i in range(step):
        r = rows + i
        left, right = [], []
        for k in range(slots):
            c = code_ref[(first + r) * slots + k]
            tile = blocks_ref[first + r, k]
            left.append(jnp.where(fields.local(c) == 1, tile, jnp.zeros_like(tile)))
            right.append(basis_ref[fields.row(c)])
        store(
            r,
            i,
            jnp.dot(jnp.concatenate(left, axis=1), jnp.concatenate(right, axis=0), preferred_element_type=F32),
        )


def smooth_first(code, half, blocks, basis, fields, step):
    rows, slots, size, _ = blocks.shape
    coarse = basis.shape[2]
    count = rows // 2
    steps = count // step

    def kernel(code_ref, half_ref, blocks_hbm, basis_hbm, out_ref, blocks_ref, basis_ref, block_sem, basis_sem):
        first = half_ref[0] * count
        rest = count - first
        load_basis = pltpu.make_async_copy(basis_hbm, basis_ref, basis_sem)
        load_basis.start()

        def load(j):
            at = pl.ds(first + j * step, step)
            return pltpu.make_async_copy(blocks_hbm.at[at], blocks_ref.at[at], block_sem.at[j])

        at = pl.ds(rest, count)
        load_rest = pltpu.make_async_copy(blocks_hbm.at[at], blocks_ref.at[at], block_sem.at[steps])
        load(0).start()
        load_basis.wait()
        ahead = min(AHEAD, steps)
        for j in range(1, ahead):
            load(j).start()

        def one_step(j, carry):
            load(j).wait()

            @pl.when(j + ahead < steps)
            def _():
                load(j + ahead).start()

            @pl.when(j + ahead == steps)
            def _():
                load_rest.start()

            def store(r, i, total):
                out_ref[r] = total.astype(BF16)

            smooth_rows(first, j * step, slots, step, code_ref, blocks_ref, basis_ref, fields, store)
            return carry

        lax.fori_loop(0, steps, one_step, 0)
        load_rest.wait()

    return pl.pallas_call(
        kernel,
        out_shape=(
            jax.ShapeDtypeStruct((count, size, coarse), BF16),
            pltpu.VMEM(blocks.shape, blocks.dtype),
            pltpu.VMEM(basis.shape, basis.dtype),
        ),
        in_specs=[smem(), smem(), hbm(), hbm()],
        out_specs=(vmem(), vmem(), vmem()),
        scratch_shapes=[pltpu.SemaphoreType.DMA((steps + 1,)), pltpu.SemaphoreType.DMA],
        compiler_params=pltpu.CompilerParams(vmem_limit_bytes=SMALL_VMEM),
        cost_estimate=cost(4 * rows * slots * size * size * coarse, rows * slots * size * size),
        name="smooth_first",
    )(code, half, in_hbm(blocks), in_hbm(basis))


def smooth_second(code, half, blocks, basis, weights, added, fields, step):
    rows, slots, size, _ = blocks.shape
    coarse = basis.shape[2]
    count = rows // 2

    def kernel(code_ref, half_ref, blocks_ref, basis_ref, weights_ref, added_ref, out_ref):
        first = half_ref[0] * count

        def one_step(j, carry):
            scale = jnp.transpose(weights_ref[pl.ds(pl.multiple_of(first + j * step, step), step), :])

            def store(r, i, total):
                out_ref[r] = (scale[:, i : i + 1] * (total + added_ref[r].astype(F32))).astype(BF16)

            smooth_rows(first, j * step, slots, step, code_ref, blocks_ref, basis_ref, fields, store)
            return carry

        lax.fori_loop(0, count // step, one_step, 0)

    return pl.pallas_call(
        kernel,
        out_shape=jax.ShapeDtypeStruct((count, size, coarse), BF16),
        in_specs=[smem(), smem(), vmem(), vmem(), vmem(), vmem()],
        out_specs=vmem(),
        compiler_params=pltpu.CompilerParams(vmem_limit_bytes=SMALL_VMEM),
        cost_estimate=cost(4 * rows * slots * size * size * coarse, rows * slots * size * size),
        name="smooth_second",
    )(code, half, in_vmem(blocks), in_vmem(basis), weights, added)


def pick_tiles(asked, own, tiles, space):
    def kernel(asked_ref, own_ref, tiles_ref, *rest):
        out_hbm, sem = rest[: space - 1], rest[-1]
        for i in range(space - 1):
            device = own_ref[0] + i + 1
            device = jnp.where(device >= space, device - space, device)
            for j in range(CAP):
                row = asked_ref[device * ASK_ROWS, j]
                pltpu.make_async_copy(tiles_ref.at[row], out_hbm[i].at[j], sem.at[i]).start()
        for i in range(space - 1):
            pltpu.make_async_copy(tiles_ref.at[pl.ds(0, CAP)], out_hbm[i], sem.at[i]).wait()

    shape = (CAP,) + tiles.shape[1:]
    return pl.pallas_call(
        kernel,
        out_shape=(pltpu.HBM(shape, tiles.dtype),) * (space - 1),
        in_specs=[smem(), smem(), vmem()],
        out_specs=(hbm(),) * (space - 1),
        scratch_shapes=[pltpu.SemaphoreType.DMA((space - 1,))],
        compiler_params=pltpu.CompilerParams(vmem_limit_bytes=SMALL_VMEM),
        cost_estimate=cost(0, 1 << 16),
        name="pick_tiles",
    )(asked, own, in_vmem(tiles))


def pick_remote_blocks(listing, blocks, after):
    most = listing.shape[0] // Listing.FIELDS

    def kernel(list_ref, blocks_hbm, after_hbm, out_ref, sem):
        del after_hbm
        entry = Listing(list_ref, most)

        def start(j):
            pltpu.make_async_copy(blocks_hbm.at[entry.row(j), entry.slot(j)], out_ref.at[j], sem).start()

        for_each(most, start)
        pltpu.make_async_copy(out_ref, out_ref, sem).wait()

    return pl.pallas_call(
        kernel,
        out_shape=pltpu.VMEM((most,) + blocks.shape[2:], blocks.dtype),
        in_specs=[smem(), hbm(), hbm()],
        out_specs=vmem(),
        scratch_shapes=[pltpu.SemaphoreType.DMA],
        compiler_params=pltpu.CompilerParams(vmem_limit_bytes=SMALL_VMEM),
        cost_estimate=cost(0, 1 << 16),
        name="pick_remote_blocks",
    )(listing, in_hbm(blocks), after)


def remote_sums(listing, tiles, received, weights):
    n = len(received)
    most, size, _ = tiles.shape
    coarse = received[0].shape[2]

    def kernel(list_ref, weights_ref, tiles_ref, *rest):
        received_refs, (out_ref, arrived) = rest[:n], rest[-2:]
        entry = Listing(list_ref, most)
        for i in range(n):
            arrived[i * CAP : (i + 1) * CAP] = received_refs[i][...]

        def one(j):
            total = jnp.dot(tiles_ref[j], arrived[entry.near_bucket(j)], preferred_element_type=F32)
            scale = weights_ref[pl.ds(entry.row(j), 1), :]
            scale = jnp.where(entry.live(j), scale, jnp.zeros_like(scale))
            scale = jnp.transpose(jnp.broadcast_to(scale, (8, size)))[:, :1]
            out_ref[j] = (total * scale).astype(BF16)

        for_each(most, one)

    return pl.pallas_call(
        kernel,
        out_shape=jax.ShapeDtypeStruct((most, size, coarse), BF16),
        in_specs=[smem(), vmem(), vmem()] + [vmem()] * n,
        out_specs=vmem(),
        scratch_shapes=[pltpu.VMEM((n * CAP, size, coarse), BF16)],
        compiler_params=pltpu.CompilerParams(vmem_limit_bytes=LARGE_VMEM),
        cost_estimate=cost(0, 1 << 16),
        name="remote_sums",
    )(listing, weights, in_vmem(tiles), *received)


def take_off(work, list_refs, sum_refs, most):
    for list_ref, sum_ref in zip(list_refs, sum_refs):
        entry = Listing(list_ref, most)

        def take(j):
            r = entry.row(j)
            work[r] = work[r] - sum_ref[j].astype(F32)

        for_each(most, take)


def local_prolong(half, basis, own, other, sums, lists):
    rows, size, coarse = basis.shape
    count = rows // 2
    n, m = len(own), len(sums)
    most = sums[0].shape[0]
    step = max(d for d in range(1, 17) if rows % d == 0)

    def kernel(half_ref, *rest):
        list_refs, basis_ref, rest = rest[:m], rest[m], rest[m + 1 :]
        out_ref, rounded_ref, rounded_hbm, sem = rest[-4:]

        def part(base, refs):
            def one(r, carry):
                total = refs[0][r].astype(F32)
                for ref in refs[1:]:
                    total = total + ref[r].astype(F32)
                out_ref[base + r] = basis_ref[base + r].astype(F32) - total
                return carry

            lax.fori_loop(0, count, one, 0, unroll=4)

        part(half_ref[0] * count, rest[:n])
        part((1 - half_ref[0]) * count, rest[n : 2 * n])
        take_off(out_ref, list_refs, rest[2 * n : 2 * n + m], most)

        def rounded(g, carry):
            for i in range(step):
                rounded_ref[g * step + i] = out_ref[g * step + i].astype(BF16)
            at = pl.ds(g * step, step)
            pltpu.make_async_copy(rounded_ref.at[at], rounded_hbm.at[at], sem).start()
            return carry

        lax.fori_loop(0, rows // step, rounded, 0)
        pltpu.make_async_copy(rounded_ref, rounded_hbm, sem).wait()

    tiles = (rows, size, coarse)
    return pl.pallas_call(
        kernel,
        out_shape=(pltpu.VMEM(tiles, F32), pltpu.VMEM(tiles, BF16), pltpu.HBM(tiles, BF16)),
        in_specs=[smem()] * (1 + m) + [vmem()] * (1 + 2 * n + m),
        out_specs=(vmem(), vmem(), hbm()),
        scratch_shapes=[pltpu.SemaphoreType.DMA],
        compiler_params=pltpu.CompilerParams(vmem_limit_bytes=LARGE_VMEM + 2 * n * rows * size * coarse),
        cost_estimate=cost(0, rows * size * coarse * 10),
        name="local_prolong",
    )(half, *lists, basis, *own, *other, *sums)


def finish_prolong(partial, rounded, sums, lists, asked, space):
    rows, size, coarse = partial.shape
    n = len(sums)
    most = sums[0].shape[0]
    count = space * CAP

    def kernel(asked_ref, *rest):
        list_refs, sum_refs, rest = rest[:n], rest[n + 2 : 2 * n + 2], rest[2 * n + 2 :]
        work, rounded_ref, send_ref, rows_ref = rest
        take_off(work, list_refs, sum_refs, most)
        for i, list_ref in enumerate(list_refs):
            entry = Listing(list_ref, most)

            def finish(j):
                tile = work[entry.row(j)].astype(BF16)
                rounded_ref[entry.row(j)] = tile
                rows_ref[i * most + j] = tile

            for_each(most, finish)
        for i in range(space):
            for j in range(CAP):
                send_ref[i * CAP + j] = rounded_ref[asked_ref[i * ASK_ROWS, j]]

    tiles = (rows, size, coarse)
    return pl.pallas_call(
        kernel,
        out_shape=(
            pltpu.VMEM(tiles, F32),
            pltpu.VMEM(tiles, BF16),
            pltpu.HBM((count, size, coarse), BF16),
            pltpu.HBM((n * most, size, coarse), BF16),
        ),
        in_specs=[smem()] * (1 + n) + [vmem()] * (2 + n),
        out_specs=(vmem(),) * 4,
        input_output_aliases={1 + n: 0, 2 + n: 1},
        compiler_params=pltpu.CompilerParams(vmem_limit_bytes=LARGE_VMEM + 4 * n * most * size * coarse + 2 * count * size * coarse),
        cost_estimate=cost(0, rows * size * coarse * 4),
        name="finish_prolong",
    )(asked, *lists, in_vmem(partial), in_vmem(rounded), *sums)[2:]


def local_coarse(code, target, listing, lists, blocks, prolong, finished, fields, targets, step):
    rows, slots, size, _ = blocks.shape
    coarse = prolong.shape[2]
    half = targets // 2
    steps = rows // step
    most = listing.shape[0] // Listing.FIELDS
    n = len(lists)

    def kernel(code_ref, target_ref, list_ref, *rest):
        list_refs, (blocks_hbm, prolong_hbm, finished_hbm) = rest[:n], rest[n : n + 3]
        keep_ref, send_ref, tiles_ref, own_ref = rest[n + 3 : n + 7]
        blocks_ref, prolong_ref, finished_ref, work, applied, sem, psem = rest[n + 7 :]
        load_prolong = pltpu.make_async_copy(prolong_hbm, prolong_ref, psem.at[0])
        load_prolong.start()
        load_finished = pltpu.make_async_copy(finished_hbm, finished_ref, psem.at[1])
        load_finished.start()

        def load(j):
            at = pl.ds(j * step, step)
            return pltpu.make_async_copy(blocks_hbm.at[at], blocks_ref.at[at], sem.at[j])

        load(0).start()
        work[...] = jnp.zeros_like(work)
        load_prolong.wait()
        load_finished.wait()
        for j in range(1, min(AHEAD, steps)):
            load(j).start()
        for i, far_ref in enumerate(list_refs):
            far = Listing(far_ref, most)

            def place(j):
                prolong_ref[far.row(j)] = finished_ref[i * most + j]

            for_each(most, place)

        def one_step(j, carry):
            load(j).wait()

            @pl.when(j + AHEAD < steps)
            def _():
                load(j + AHEAD).start()

            for i in range(step):
                for k in range(slots):
                    c = code_ref[(j * step + i) * slots + k]
                    tile = blocks_ref[j * step + i, k]
                    tile = jnp.where(fields.local(c) == 1, tile, jnp.zeros_like(tile))
                    applied[i, :, k * coarse : (k + 1) * coarse] = jnp.dot(
                        tile, prolong_ref[fields.row(c)], preferred_element_type=F32
                    ).astype(BF16)
            for i in range(step):
                given = lax.dot_general(
                    prolong_ref[j * step + i], applied[i], (((0,), (0,)), ((), ())), preferred_element_type=F32
                )
                for k in range(slots):
                    at = target_ref[(j * step + i) * slots + k]
                    work[at] += given[:, k * coarse : (k + 1) * coarse]
            return carry

        lax.fori_loop(0, steps, one_step, 0)
        keep_ref[...] = work[pl.ds(0, half)]
        send_ref[...] = work[pl.ds(half, half)]
        entry = Listing(list_ref, most)

        def pick(j):
            tiles_ref[j] = blocks_ref[entry.row(j), entry.slot(j)]
            own_ref[j] = prolong_ref[entry.row(j)]

        for_each(most, pick)

    out = (half, coarse, coarse)
    return pl.pallas_call(
        kernel,
        out_shape=(
            pltpu.HBM(out, F32),
            pltpu.HBM(out, F32),
            pltpu.HBM((most, size, size), BF16),
            pltpu.HBM((most, size, coarse), BF16),
        ),
        in_specs=[smem()] * (3 + n) + [hbm()] * 3,
        out_specs=(vmem(),) * 4,
        scratch_shapes=[
            pltpu.VMEM(blocks.shape, BF16),
            pltpu.VMEM(prolong.shape, BF16),
            pltpu.VMEM(finished.shape, BF16),
            pltpu.VMEM((targets, coarse, coarse), F32),
            pltpu.VMEM((step, size, slots * coarse), BF16),
            pltpu.SemaphoreType.DMA((steps,)),
            pltpu.SemaphoreType.DMA((2,)),
        ],
        compiler_params=pltpu.CompilerParams(vmem_limit_bytes=36 << 20),
        cost_estimate=cost(8 * rows * slots * size * size * coarse, 2 * rows * slots * size * size),
        name="local_coarse",
    )(code, target, listing, *lists, in_hbm(blocks), in_hbm(prolong), in_hbm(finished))


def remote_coarse(listing, tiles, own, received):
    most, size, coarse = own.shape

    def kernel(list_ref, tiles_hbm, own_hbm, received_ref, out_ref, applied, tiles_ref, own_ref, sem):
        load_tiles = pltpu.make_async_copy(tiles_hbm, tiles_ref, sem.at[0])
        load_own = pltpu.make_async_copy(own_hbm, own_ref, sem.at[1])
        load_tiles.start()
        load_own.start()
        entry = Listing(list_ref, most)

        def apply(j):
            applied[j] = jnp.dot(tiles_ref[j], received_ref[entry.bucket(j)], preferred_element_type=F32).astype(BF16)

        def give(j):
            given = lax.dot_general(own_ref[j], applied[j], (((0,), (0,)), ((), ())), preferred_element_type=F32)
            out_ref[j] = jnp.where(entry.live(j), given, jnp.zeros_like(given)).astype(BF16)

        load_tiles.wait()
        for_each(most, apply)
        load_own.wait()
        for_each(most, give)

    return pl.pallas_call(
        kernel,
        out_shape=jax.ShapeDtypeStruct((most, coarse, coarse), BF16),
        in_specs=[smem(), hbm(), hbm(), vmem()],
        out_specs=vmem(),
        scratch_shapes=[
            pltpu.VMEM((most, size, coarse), BF16),
            pltpu.VMEM((most, size, size), BF16),
            pltpu.VMEM((most, size, coarse), BF16),
            pltpu.SemaphoreType.DMA((2,)),
        ],
        compiler_params=pltpu.CompilerParams(vmem_limit_bytes=SMALL_VMEM),
        cost_estimate=cost(4 * most * size * size * coarse, 8 << 20),
        name="remote_coarse",
    )(listing, in_hbm(tiles), in_hbm(own), received)


def share_sums(chip, kept, arrived, target, listing, given, sibling_target, sibling_listing, sibling_given, chips):
    half, coarse, _ = kept.shape
    share = half // chips
    most = given.shape[0]

    def kernel(chip_ref, target_ref, list_ref, sibling_target_ref, sibling_ref, *rest):
        kept_ref, arrived_ref, given_ref, sibling_given_ref, own_ref = rest[:5]
        send_refs, work = rest[5:-1], rest[-1]
        work[...] = kept_ref[...] + arrived_ref[...]
        own_entry, sibling_entry = Listing(list_ref, most), Listing(sibling_ref, most)

        def add_own(j):
            at = target_ref[own_entry.place(j)]

            @pl.when(at < half)
            def _():
                work[at] += given_ref[j].astype(F32)

        def add_sibling(j):
            at_sibling = sibling_target_ref[sibling_entry.place(j)]

            @pl.when(at_sibling >= half)
            def _():
                work[at_sibling - half] += sibling_given_ref[j].astype(F32)

        for_each(most, add_own)
        for_each(most, add_sibling)
        for j in range(chips):
            at = chip_ref[0] + j
            at = jnp.where(at >= chips, at - chips, at)
            total = work[pl.ds(at * share, share)]
            if j == 0:
                own_ref[...] = total
            else:
                send_refs[j - 1][...] = total.astype(BF16)

    tile = (share, coarse, coarse)
    return pl.pallas_call(
        kernel,
        out_shape=(jax.ShapeDtypeStruct(tile, F32),) + (jax.ShapeDtypeStruct(tile, BF16),) * (chips - 1),
        in_specs=[smem()] * 5 + [vmem()] * 4,
        out_specs=(vmem(),) * chips,
        scratch_shapes=[pltpu.VMEM(kept.shape, F32)],
        compiler_params=pltpu.CompilerParams(vmem_limit_bytes=SMALL_VMEM),
        cost_estimate=cost(0, kept.size * 12),
        name="share_sums",
    )(chip, target, listing, sibling_target, sibling_listing, kept, arrived, given, sibling_given)


def permute_order(space):
    first = [space // 2, space - 2, space - 1]
    return first + [j for j in range(1, space) if j not in first]


def per_device(blocks, basis_tiles, weights, neighbour_device, neighbour_row, counts, aggregate, pair_slot):
    space = lax.axis_size("space")
    cols = lax.axis_size("col")
    chips = cols // 2
    own_index = lax.axis_index("space")
    col_index = lax.axis_index("col")
    rows, slots = neighbour_device.shape
    targets = NCD * KC
    share = targets // cols
    most = min(STATED_REMOTE.get(space, CAP * (space - 1)), rows * slots)
    half_rows = rows // 2
    step = max(s for s in (1, 2, 4, 8) if half_rows % s == 0)
    fields = Fields(rows)

    core_index = col_index % 2
    core = core_index.reshape(1).astype(jnp.int32)
    chip = (col_index // 2).reshape(1).astype(jnp.int32)
    own = own_index.reshape(1).astype(jnp.int32)

    def to_sibling(x):
        return lax.ppermute(x, "col", [(i, i ^ 1) for i in range(cols)])

    def to_chip(x, j):
        return lax.ppermute(x, "col", [(i, (i + 2 * j) % cols) for i in range(cols)])

    def to_distance(x, j):
        return lax.ppermute(x, "space", [(i, (i + j) % space) for i in range(space)])

    def to_owner(x):
        return lax.all_to_all(x, "space", split_axis=0, concat_axis=0, tiled=True)

    slot_number = col_index * slots + jnp.arange(slots, dtype=jnp.int32)
    live = slot_number[None, :] < counts[:, None]
    far = neighbour_device != own_index
    target = aggregate[:, None] * KC + pair_slot
    owner = target // share
    target = (owner % 2 != core_index) * (targets // 2) + (owner // 2) * share + target % share
    target = target.astype(jnp.int32).reshape(rows * slots)
    code = fields.pack(neighbour_row, live & ~far, live & far, neighbour_device).reshape(rows * slots)

    sent_half, near_blocks, near_basis = smooth_first(code, 1 - core, blocks, basis_tiles, fields, step)
    ask, listing = list_remote(code, own, sent_half, fields, rows, slots, space, most)
    lists = [listing] + [to_chip(listing, j) for j in range(1, chips)]
    sibling_sum, ask = lax.optimization_barrier((to_sibling(sent_half), ask))
    kept_half = smooth_second(code, core, near_blocks, near_basis, weights, sibling_sum, fields, step)
    kept_half, *lists = lax.optimization_barrier((kept_half, *lists))
    far_half = [to_chip(kept_half, j) for j in range(1, chips)]

    sibling_lists = [to_sibling(x) for x in lists]
    asked, sibling_lists, target, sibling_target = lax.optimization_barrier(
        (to_owner(ask), sibling_lists, target, to_sibling(target))
    )
    picked = pick_tiles(asked, own, near_basis, space)
    order = permute_order(space)
    received = {}
    for at, j in enumerate(order):
        x = picked[j - 1]
        if at >= IN_FLIGHT:
            before = order[at - IN_FLIGHT]
            x, received[before] = lax.optimization_barrier((x, received[before]))
        received[j] = to_distance(x, j)
    received = [received[j] for j in range(1, space)]
    remote_blocks = pick_remote_blocks(listing, blocks, received[len(received) // 2])
    far_half, received, remote_blocks = lax.optimization_barrier((far_half, received, remote_blocks))
    own_half = [kept_half] + far_half
    other_half = [to_sibling(x) for x in own_half]
    own_sums = remote_sums(listing, remote_blocks, received, weights)
    far_sums = [to_chip(own_sums, j) for j in range(1, chips)]
    near_sums = [own_sums, to_sibling(own_sums)]
    partial, rounded, prolong = local_prolong(
        core, basis_tiles, own_half, other_half, near_sums, [listing, sibling_lists[0]]
    )
    partial, rounded, *far_sums = lax.optimization_barrier((partial, rounded, *far_sums))
    far_sums += [to_sibling(x) for x in far_sums]
    far_lists = lists[1:] + sibling_lists[1:]
    sent, finished = finish_prolong(partial, rounded, far_sums, far_lists, asked, space)

    received_prolong = to_owner(sent)
    keep, send, remote_blocks, own_tiles = local_coarse(
        code, target, listing, far_lists, blocks, prolong, finished, fields, targets, step
    )
    arrived = to_sibling(send)
    given = remote_coarse(listing, remote_blocks, own_tiles, received_prolong)
    sibling_given = to_sibling(given)
    total, *rest = share_sums(
        chip, keep, arrived, target, listing, given, sibling_target, sibling_lists[0], sibling_given, chips
    )
    for j, part in enumerate(rest, 1):
        total = total + to_chip(part, j).astype(F32)
    return total


def solution(mesh):
    return jax.shard_map(
        per_device,
        mesh=mesh,
        in_specs=(
            P("space", "col", None, None),
            P("space", None, None),
            P("space", None),
            P("space", "col"),
            P("space", "col"),
            P("space"),
            P("space"),
            P("space", "col"),
        ),
        out_specs=P(("space", "col"), None, None),
        check_vma=False,
    )
```

```python
import jax
import jax.numpy as jnp
from jax import lax
from jax.experimental import pallas as pl
from jax.experimental.pallas import tpu as pltpu
from jax.sharding import PartitionSpec as P

KC = 4
CAP = 3
NCD = 10
STATED_REMOTE = {8: 15, 32: 60}

F32 = jnp.float32
BF16 = jnp.bfloat16
AHEAD = 3
IN_FLIGHT = 4
SMALL_VMEM = 6 << 20
LARGE_VMEM = 12 << 20
LANES = 128
ASK_ROWS = 8


def vmem():
    return pl.BlockSpec(memory_space=pltpu.VMEM)


def smem():
    return pl.BlockSpec(memory_space=pltpu.SMEM)


def for_each(n, body):
    if n <= 24:
        for j in range(n):
            body(j)
    else:
        lax.fori_loop(0, n, lambda j, carry: (body(j), carry)[1], 0, unroll=4)


def in_hbm(x):
    return pltpu.with_memory_space_constraint(x, pltpu.HBM)


def in_vmem(x):
    return pltpu.with_memory_space_constraint(x, pltpu.VMEM)


def hbm():
    return pl.BlockSpec(memory_space=pl.ANY)


def cost(flops, bytes_accessed):
    return pl.CostEstimate(flops=int(flops), bytes_accessed=int(bytes_accessed), transcendentals=0)


class Fields:
    def __init__(self, rows):
        self.row_bits = max(1, (rows - 1).bit_length())
        self.local_at = self.row_bits
        self.remote_at = self.row_bits + 1
        self.device_at = self.row_bits + 2

    def pack(self, row, local, remote, device):
        return (
            row
            + local.astype(jnp.int32) * (1 << self.local_at)
            + remote.astype(jnp.int32) * (1 << self.remote_at)
            + device * (1 << self.device_at)
        )

    def row(self, code):
        return code & ((1 << self.row_bits) - 1)

    def local(self, code):
        return (code >> self.local_at) & 1

    def remote(self, code):
        return (code >> self.remote_at) & 1

    def device(self, code):
        return code >> self.device_at


def list_remote(code, own, after, fields, rows, slots, space, most):
    def kernel(code_ref, own_ref, after_ref, ask_ref, list_ref, used, found):
        del after_ref
        for i in range(space):
            used[i] = 0
            for j in range(CAP):
                ask_ref[i * ASK_ROWS, j] = 0

        def clear(i, carry):
            list_ref[i] = 0
            return carry

        lax.fori_loop(0, Listing.FIELDS * most, clear, 0, unroll=10)

        def look(r, count):
            for k in range(slots):
                found[count] = r * slots + k
                count = count + fields.remote(code_ref[r * slots + k])
            return count

        count = lax.fori_loop(0, rows, look, jnp.int32(0), unroll=8)

        def enter(n, carry):
            at = found[n]
            c = code_ref[at]
            row = lax.div(at, slots)
            device = fields.device(c)
            place = used[device]
            used[device] = place + 1
            ask_ref[device * ASK_ROWS, place] = fields.row(c)
            gap = own_ref[0] - device
            gap = jnp.where(gap < 0, gap + space, gap)
            list_ref[n] = row
            list_ref[most + n] = at - row * slots
            list_ref[2 * most + n] = device * CAP + place
            list_ref[3 * most + n] = at
            list_ref[4 * most + n] = 1
            list_ref[5 * most + n] = (gap - 1) * CAP + place
            return carry

        lax.fori_loop(0, count, enter, 0)

    return pl.pallas_call(
        kernel,
        out_shape=(
            jax.ShapeDtypeStruct((space * ASK_ROWS, LANES), jnp.int32),
            jax.ShapeDtypeStruct((Listing.FIELDS * most,), jnp.int32),
        ),
        in_specs=[smem(), smem(), hbm()],
        out_specs=(smem(), smem()),
        scratch_shapes=[pltpu.SMEM((space,), jnp.int32), pltpu.SMEM((rows * slots + 1,), jnp.int32)],
        compiler_params=pltpu.CompilerParams(vmem_limit_bytes=SMALL_VMEM),
        cost_estimate=cost(0, 8 << 20),
        name="list_remote",
    )(code, own, after)


class Listing:
    FIELDS = 6

    def __init__(self, ref, most):
        self.row = lambda j: ref[j]
        self.slot = lambda j: ref[most + j]
        self.bucket = lambda j: ref[2 * most + j]
        self.place = lambda j: ref[3 * most + j]
        self.live = lambda j: ref[4 * most + j] == 1
        self.near_bucket = lambda j: ref[5 * most + j]


def smooth_rows(first, rows, slots, step, code_ref, blocks_ref, basis_ref, fields, store):
    for i in range(step):
        r = rows + i
        left, right = [], []
        for k in range(slots):
            c = code_ref[(first + r) * slots + k]
            tile = blocks_ref[first + r, k]
            left.append(jnp.where(fields.local(c) == 1, tile, jnp.zeros_like(tile)))
            right.append(basis_ref[fields.row(c)])
        store(
            r,
            i,
            jnp.dot(jnp.concatenate(left, axis=1), jnp.concatenate(right, axis=0), preferred_element_type=F32),
        )


def smooth_first(code, half, blocks, basis, fields, step):
    rows, slots, size, _ = blocks.shape
    coarse = basis.shape[2]
    count = rows // 2
    steps = count // step

    def kernel(code_ref, half_ref, blocks_hbm, basis_hbm, out_ref, blocks_ref, basis_ref, block_sem, basis_sem):
        first = half_ref[0] * count
        rest = count - first
        load_basis = pltpu.make_async_copy(basis_hbm, basis_ref, basis_sem)
        load_basis.start()

        def load(j):
            at = pl.ds(first + j * step, step)
            return pltpu.make_async_copy(blocks_hbm.at[at], blocks_ref.at[at], block_sem.at[j])

        at = pl.ds(rest, count)
        load_rest = pltpu.make_async_copy(blocks_hbm.at[at], blocks_ref.at[at], block_sem.at[steps])
        load(0).start()
        load_basis.wait()
        ahead = min(AHEAD, steps)
        for j in range(1, ahead):
            load(j).start()

        def one_step(j, carry):
            load(j).wait()

            @pl.when(j + ahead < steps)
            def _():
                load(j + ahead).start()

            @pl.when(j + ahead == steps)
            def _():
                load_rest.start()

            def store(r, i, total):
                out_ref[r] = total.astype(BF16)

            smooth_rows(first, j * step, slots, step, code_ref, blocks_ref, basis_ref, fields, store)
            return carry

        lax.fori_loop(0, steps, one_step, 0)
        load_rest.wait()

    return pl.pallas_call(
        kernel,
        out_shape=(
            jax.ShapeDtypeStruct((count, size, coarse), BF16),
            pltpu.VMEM(blocks.shape, blocks.dtype),
            pltpu.VMEM(basis.shape, basis.dtype),
        ),
        in_specs=[smem(), smem(), hbm(), hbm()],
        out_specs=(vmem(), vmem(), vmem()),
        scratch_shapes=[pltpu.SemaphoreType.DMA((steps + 1,)), pltpu.SemaphoreType.DMA],
        compiler_params=pltpu.CompilerParams(vmem_limit_bytes=SMALL_VMEM),
        cost_estimate=cost(4 * rows * slots * size * size * coarse, rows * slots * size * size),
        name="smooth_first",
    )(code, half, in_hbm(blocks), in_hbm(basis))


def smooth_second(code, half, blocks, basis, weights, added, fields, step):
    rows, slots, size, _ = blocks.shape
    coarse = basis.shape[2]
    count = rows // 2

    def kernel(code_ref, half_ref, blocks_ref, basis_ref, weights_ref, added_ref, out_ref):
        first = half_ref[0] * count

        def one_step(j, carry):
            scale = jnp.transpose(weights_ref[pl.ds(pl.multiple_of(first + j * step, step), step), :])

            def store(r, i, total):
                out_ref[r] = (scale[:, i : i + 1] * (total + added_ref[r].astype(F32))).astype(BF16)

            smooth_rows(first, j * step, slots, step, code_ref, blocks_ref, basis_ref, fields, store)
            return carry

        lax.fori_loop(0, count // step, one_step, 0)

    return pl.pallas_call(
        kernel,
        out_shape=jax.ShapeDtypeStruct((count, size, coarse), BF16),
        in_specs=[smem(), smem(), vmem(), vmem(), vmem(), vmem()],
        out_specs=vmem(),
        compiler_params=pltpu.CompilerParams(vmem_limit_bytes=SMALL_VMEM),
        cost_estimate=cost(4 * rows * slots * size * size * coarse, rows * slots * size * size),
        name="smooth_second",
    )(code, half, in_vmem(blocks), in_vmem(basis), weights, added)


def pick_tiles(asked, own, tiles, space):
    def kernel(asked_ref, own_ref, tiles_ref, *rest):
        out_hbm, sem = rest[: space - 1], rest[-1]
        for i in range(space - 1):
            device = own_ref[0] + i + 1
            device = jnp.where(device >= space, device - space, device)
            for j in range(CAP):
                row = asked_ref[device * ASK_ROWS, j]
                pltpu.make_async_copy(tiles_ref.at[row], out_hbm[i].at[j], sem.at[i]).start()
        for i in range(space - 1):
            pltpu.make_async_copy(tiles_ref.at[pl.ds(0, CAP)], out_hbm[i], sem.at[i]).wait()

    shape = (CAP,) + tiles.shape[1:]
    return pl.pallas_call(
        kernel,
        out_shape=(pltpu.HBM(shape, tiles.dtype),) * (space - 1),
        in_specs=[smem(), smem(), vmem()],
        out_specs=(hbm(),) * (space - 1),
        scratch_shapes=[pltpu.SemaphoreType.DMA((space - 1,))],
        compiler_params=pltpu.CompilerParams(vmem_limit_bytes=SMALL_VMEM),
        cost_estimate=cost(0, 1 << 16),
        name="pick_tiles",
    )(asked, own, in_vmem(tiles))


def pick_remote_blocks(listing, blocks, after):
    most = listing.shape[0] // Listing.FIELDS

    def kernel(list_ref, blocks_hbm, after_hbm, out_ref, sem):
        del after_hbm
        entry = Listing(list_ref, most)

        def start(j):
            pltpu.make_async_copy(blocks_hbm.at[entry.row(j), entry.slot(j)], out_ref.at[j], sem).start()

        for_each(most, start)
        pltpu.make_async_copy(out_ref, out_ref, sem).wait()

    return pl.pallas_call(
        kernel,
        out_shape=pltpu.VMEM((most,) + blocks.shape[2:], blocks.dtype),
        in_specs=[smem(), hbm(), hbm()],
        out_specs=vmem(),
        scratch_shapes=[pltpu.SemaphoreType.DMA],
        compiler_params=pltpu.CompilerParams(vmem_limit_bytes=SMALL_VMEM),
        cost_estimate=cost(0, 1 << 16),
        name="pick_remote_blocks",
    )(listing, in_hbm(blocks), after)


def remote_sums(listing, tiles, received, weights):
    n = len(received)
    most, size, _ = tiles.shape
    coarse = received[0].shape[2]

    def kernel(list_ref, weights_ref, tiles_ref, *rest):
        received_refs, (out_ref, arrived) = rest[:n], rest[-2:]
        entry = Listing(list_ref, most)
        for i in range(n):
            arrived[i * CAP : (i + 1) * CAP] = received_refs[i][...]

        def one(j):
            total = jnp.dot(tiles_ref[j], arrived[entry.near_bucket(j)], preferred_element_type=F32)
            scale = weights_ref[pl.ds(entry.row(j), 1), :]
            scale = jnp.where(entry.live(j), scale, jnp.zeros_like(scale))
            scale = jnp.transpose(jnp.broadcast_to(scale, (8, size)))[:, :1]
            out_ref[j] = (total * scale).astype(BF16)

        for_each(most, one)

    return pl.pallas_call(
        kernel,
        out_shape=jax.ShapeDtypeStruct((most, size, coarse), BF16),
        in_specs=[smem(), vmem(), vmem()] + [vmem()] * n,
        out_specs=vmem(),
        scratch_shapes=[pltpu.VMEM((n * CAP, size, coarse), BF16)],
        compiler_params=pltpu.CompilerParams(vmem_limit_bytes=LARGE_VMEM),
        cost_estimate=cost(0, 1 << 16),
        name="remote_sums",
    )(listing, weights, in_vmem(tiles), *received)


def take_off(work, list_refs, sum_refs, most):
    for list_ref, sum_ref in zip(list_refs, sum_refs):
        entry = Listing(list_ref, most)

        def take(j):
            r = entry.row(j)
            work[r] = work[r] - sum_ref[j].astype(F32)

        for_each(most, take)


def local_prolong(half, basis, own, other, sums, lists):
    rows, size, coarse = basis.shape
    count = rows // 2
    n, m = len(own), len(sums)
    most = sums[0].shape[0]
    step = max(d for d in range(1, 17) if rows % d == 0)

    def kernel(half_ref, *rest):
        list_refs, basis_ref, rest = rest[:m], rest[m], rest[m + 1 :]
        out_ref, rounded_ref, rounded_hbm, sem = rest[-4:]

        def part(base, refs):
            def one(r, carry):
                total = refs[0][r].astype(F32)
                for ref in refs[1:]:
                    total = total + ref[r].astype(F32)
                out_ref[base + r] = basis_ref[base + r].astype(F32) - total
                return carry

            lax.fori_loop(0, count, one, 0, unroll=4)

        part(half_ref[0] * count, rest[:n])
        part((1 - half_ref[0]) * count, rest[n : 2 * n])
        take_off(out_ref, list_refs, rest[2 * n : 2 * n + m], most)

        def rounded(g, carry):
            for i in range(step):
                rounded_ref[g * step + i] = out_ref[g * step + i].astype(BF16)
            at = pl.ds(g * step, step)
            pltpu.make_async_copy(rounded_ref.at[at], rounded_hbm.at[at], sem).start()
            return carry

        lax.fori_loop(0, rows // step, rounded, 0)
        pltpu.make_async_copy(rounded_ref, rounded_hbm, sem).wait()

    tiles = (rows, size, coarse)
    return pl.pallas_call(
        kernel,
        out_shape=(pltpu.VMEM(tiles, F32), pltpu.VMEM(tiles, BF16), pltpu.HBM(tiles, BF16)),
        in_specs=[smem()] * (1 + m) + [vmem()] * (1 + 2 * n + m),
        out_specs=(vmem(), vmem(), hbm()),
        scratch_shapes=[pltpu.SemaphoreType.DMA],
        compiler_params=pltpu.CompilerParams(vmem_limit_bytes=LARGE_VMEM + 2 * n * rows * size * coarse),
        cost_estimate=cost(0, rows * size * coarse * 10),
        name="local_prolong",
    )(half, *lists, basis, *own, *other, *sums)


def finish_prolong(partial, rounded, sums, lists, asked, space):
    rows, size, coarse = partial.shape
    n = len(sums)
    most = sums[0].shape[0]
    count = space * CAP

    def kernel(asked_ref, *rest):
        list_refs, sum_refs, rest = rest[:n], rest[n + 2 : 2 * n + 2], rest[2 * n + 2 :]
        work, rounded_ref, send_ref, rows_ref = rest
        take_off(work, list_refs, sum_refs, most)
        for i, list_ref in enumerate(list_refs):
            entry = Listing(list_ref, most)

            def finish(j):
                tile = work[entry.row(j)].astype(BF16)
                rounded_ref[entry.row(j)] = tile
                rows_ref[i * most + j] = tile

            for_each(most, finish)
        for i in range(space):
            for j in range(CAP):
                send_ref[i * CAP + j] = rounded_ref[asked_ref[i * ASK_ROWS, j]]

    tiles = (rows, size, coarse)
    return pl.pallas_call(
        kernel,
        out_shape=(
            pltpu.VMEM(tiles, F32),
            pltpu.VMEM(tiles, BF16),
            pltpu.HBM((count, size, coarse), BF16),
            pltpu.HBM((n * most, size, coarse), BF16),
        ),
        in_specs=[smem()] * (1 + n) + [vmem()] * (2 + n),
        out_specs=(vmem(),) * 4,
        input_output_aliases={1 + n: 0, 2 + n: 1},
        compiler_params=pltpu.CompilerParams(vmem_limit_bytes=LARGE_VMEM + 4 * n * most * size * coarse + 2 * count * size * coarse),
        cost_estimate=cost(0, rows * size * coarse * 4),
        name="finish_prolong",
    )(asked, *lists, in_vmem(partial), in_vmem(rounded), *sums)[2:]


def local_coarse(code, target, listing, lists, blocks, prolong, finished, fields, targets, step):
    rows, slots, size, _ = blocks.shape
    coarse = prolong.shape[2]
    half = targets // 2
    steps = rows // step
    most = listing.shape[0] // Listing.FIELDS
    n = len(lists)

    def kernel(code_ref, target_ref, list_ref, *rest):
        list_refs, (blocks_hbm, prolong_hbm, finished_hbm) = rest[:n], rest[n : n + 3]
        keep_ref, send_ref, tiles_ref, own_ref = rest[n + 3 : n + 7]
        blocks_ref, prolong_ref, finished_ref, work, applied, sem, psem = rest[n + 7 :]
        load_prolong = pltpu.make_async_copy(prolong_hbm, prolong_ref, psem.at[0])
        load_prolong.start()
        load_finished = pltpu.make_async_copy(finished_hbm, finished_ref, psem.at[1])
        load_finished.start()

        def load(j):
            at = pl.ds(j * step, step)
            return pltpu.make_async_copy(blocks_hbm.at[at], blocks_ref.at[at], sem.at[j])

        load(0).start()
        work[...] = jnp.zeros_like(work)
        load_prolong.wait()
        load_finished.wait()
        for j in range(1, min(AHEAD, steps)):
            load(j).start()
        for i, far_ref in enumerate(list_refs):
            far = Listing(far_ref, most)

            def place(j):
                prolong_ref[far.row(j)] = finished_ref[i * most + j]

            for_each(most, place)

        def one_step(j, carry):
            load(j).wait()

            @pl.when(j + AHEAD < steps)
            def _():
                load(j + AHEAD).start()

            for i in range(step):
                for k in range(slots):
                    c = code_ref[(j * step + i) * slots + k]
                    tile = blocks_ref[j * step + i, k]
                    tile = jnp.where(fields.local(c) == 1, tile, jnp.zeros_like(tile))
                    applied[i, :, k * coarse : (k + 1) * coarse] = jnp.dot(
                        tile, prolong_ref[fields.row(c)], preferred_element_type=F32
                    ).astype(BF16)
            for i in range(step):
                given = lax.dot_general(
                    prolong_ref[j * step + i], applied[i], (((0,), (0,)), ((), ())), preferred_element_type=F32
                )
                for k in range(slots):
                    at = target_ref[(j * step + i) * slots + k]
                    work[at] += given[:, k * coarse : (k + 1) * coarse]
            return carry

        lax.fori_loop(0, steps, one_step, 0)
        keep_ref[...] = work[pl.ds(0, half)]
        send_ref[...] = work[pl.ds(half, half)]
        entry = Listing(list_ref, most)

        def pick(j):
            tiles_ref[j] = blocks_ref[entry.row(j), entry.slot(j)]
            own_ref[j] = prolong_ref[entry.row(j)]

        for_each(most, pick)

    out = (half, coarse, coarse)
    return pl.pallas_call(
        kernel,
        out_shape=(
            pltpu.HBM(out, F32),
            pltpu.HBM(out, F32),
            pltpu.HBM((most, size, size), BF16),
            pltpu.HBM((most, size, coarse), BF16),
        ),
        in_specs=[smem()] * (3 + n) + [hbm()] * 3,
        out_specs=(vmem(),) * 4,
        scratch_shapes=[
            pltpu.VMEM(blocks.shape, BF16),
            pltpu.VMEM(prolong.shape, BF16),
            pltpu.VMEM(finished.shape, BF16),
            pltpu.VMEM((targets, coarse, coarse), F32),
            pltpu.VMEM((step, size, slots * coarse), BF16),
            pltpu.SemaphoreType.DMA((steps,)),
            pltpu.SemaphoreType.DMA((2,)),
        ],
        compiler_params=pltpu.CompilerParams(vmem_limit_bytes=36 << 20),
        cost_estimate=cost(8 * rows * slots * size * size * coarse, 2 * rows * slots * size * size),
        name="local_coarse",
    )(code, target, listing, *lists, in_hbm(blocks), in_hbm(prolong), in_hbm(finished))


def remote_coarse(listing, tiles, own, received):
    most, size, coarse = own.shape

    def kernel(list_ref, tiles_hbm, own_hbm, received_ref, out_ref, applied, tiles_ref, own_ref, sem):
        load_tiles = pltpu.make_async_copy(tiles_hbm, tiles_ref, sem.at[0])
        load_own = pltpu.make_async_copy(own_hbm, own_ref, sem.at[1])
        load_tiles.start()
        load_own.start()
        entry = Listing(list_ref, most)

        def apply(j):
            applied[j] = jnp.dot(tiles_ref[j], received_ref[entry.bucket(j)], preferred_element_type=F32).astype(BF16)

        def give(j):
            given = lax.dot_general(own_ref[j], applied[j], (((0,), (0,)), ((), ())), preferred_element_type=F32)
            out_ref[j] = jnp.where(entry.live(j), given, jnp.zeros_like(given)).astype(BF16)

        load_tiles.wait()
        for_each(most, apply)
        load_own.wait()
        for_each(most, give)

    return pl.pallas_call(
        kernel,
        out_shape=jax.ShapeDtypeStruct((most, coarse, coarse), BF16),
        in_specs=[smem(), hbm(), hbm(), vmem()],
        out_specs=vmem(),
        scratch_shapes=[
            pltpu.VMEM((most, size, coarse), BF16),
            pltpu.VMEM((most, size, size), BF16),
            pltpu.VMEM((most, size, coarse), BF16),
            pltpu.SemaphoreType.DMA((2,)),
        ],
        compiler_params=pltpu.CompilerParams(vmem_limit_bytes=SMALL_VMEM),
        cost_estimate=cost(4 * most * size * size * coarse, 8 << 20),
        name="remote_coarse",
    )(listing, in_hbm(tiles), in_hbm(own), received)


def share_sums(chip, kept, arrived, target, listing, given, sibling_target, sibling_listing, sibling_given, chips):
    half, coarse, _ = kept.shape
    share = half // chips
    most = given.shape[0]

    def kernel(chip_ref, target_ref, list_ref, sibling_target_ref, sibling_ref, *rest):
        kept_ref, arrived_ref, given_ref, sibling_given_ref, own_ref = rest[:5]
        send_refs, work = rest[5:-1], rest[-1]
        work[...] = kept_ref[...] + arrived_ref[...]
        own_entry, sibling_entry = Listing(list_ref, most), Listing(sibling_ref, most)

        def add_own(j):
            at = target_ref[own_entry.place(j)]

            @pl.when(at < half)
            def _():
                work[at] += given_ref[j].astype(F32)

        def add_sibling(j):
            at_sibling = sibling_target_ref[sibling_entry.place(j)]

            @pl.when(at_sibling >= half)
            def _():
                work[at_sibling - half] += sibling_given_ref[j].astype(F32)

        for_each(most, add_own)
        for_each(most, add_sibling)
        for j in range(chips):
            at = chip_ref[0] + j
            at = jnp.where(at >= chips, at - chips, at)
            total = work[pl.ds(at * share, share)]
            if j == 0:
                own_ref[...] = total
            else:
                send_refs[j - 1][...] = total.astype(BF16)

    tile = (share, coarse, coarse)
    return pl.pallas_call(
        kernel,
        out_shape=(jax.ShapeDtypeStruct(tile, F32),) + (jax.ShapeDtypeStruct(tile, BF16),) * (chips - 1),
        in_specs=[smem()] * 5 + [vmem()] * 4,
        out_specs=(vmem(),) * chips,
        scratch_shapes=[pltpu.VMEM(kept.shape, F32)],
        compiler_params=pltpu.CompilerParams(vmem_limit_bytes=SMALL_VMEM),
        cost_estimate=cost(0, kept.size * 12),
        name="share_sums",
    )(chip, target, listing, sibling_target, sibling_listing, kept, arrived, given, sibling_given)


def permute_order(space):
    first = [space // 2, space - 2, space - 1]
    return first + [j for j in range(1, space) if j not in first]


def per_device(blocks, basis_tiles, weights, neighbour_device, neighbour_row, counts, aggregate, pair_slot):
    space = lax.axis_size("space")
    cols = lax.axis_size("col")
    chips = cols // 2
    own_index = lax.axis_index("space")
    col_index = lax.axis_index("col")
    rows, slots = neighbour_device.shape
    targets = NCD * KC
    share = targets // cols
    most = min(STATED_REMOTE.get(space, CAP * (space - 1)), rows * slots)
    half_rows = rows // 2
    step = max(s for s in (1, 2, 4, 8) if half_rows % s == 0)
    fields = Fields(rows)

    core_index = col_index % 2
    core = core_index.reshape(1).astype(jnp.int32)
    chip = (col_index // 2).reshape(1).astype(jnp.int32)
    own = own_index.reshape(1).astype(jnp.int32)

    def to_sibling(x):
        return lax.ppermute(x, "col", [(i, i ^ 1) for i in range(cols)])

    def to_chip(x, j):
        return lax.ppermute(x, "col", [(i, (i + 2 * j) % cols) for i in range(cols)])

    def to_distance(x, j):
        return lax.ppermute(x, "space", [(i, (i + j) % space) for i in range(space)])

    def to_owner(x):
        return lax.all_to_all(x, "space", split_axis=0, concat_axis=0, tiled=True)

    slot_number = col_index * slots + jnp.arange(slots, dtype=jnp.int32)
    live = slot_number[None, :] < counts[:, None]
    far = neighbour_device != own_index
    target = aggregate[:, None] * KC + pair_slot
    owner = target // share
    target = (owner % 2 != core_index) * (targets // 2) + (owner // 2) * share + target % share
    target = target.astype(jnp.int32).reshape(rows * slots)
    code = fields.pack(neighbour_row, live & ~far, live & far, neighbour_device).reshape(rows * slots)

    sent_half, near_blocks, near_basis = smooth_first(code, 1 - core, blocks, basis_tiles, fields, step)
    ask, listing = list_remote(code, own, sent_half, fields, rows, slots, space, most)
    lists = [listing] + [to_chip(listing, j) for j in range(1, chips)]
    sibling_sum, ask = lax.optimization_barrier((to_sibling(sent_half), ask))
    kept_half = smooth_second(code, core, near_blocks, near_basis, weights, sibling_sum, fields, half_rows)
    kept_half, *lists = lax.optimization_barrier((kept_half, *lists))
    far_half = [to_chip(kept_half, j) for j in range(1, chips)]

    sibling_lists = [to_sibling(x) for x in lists]
    asked, sibling_lists, target, sibling_target = lax.optimization_barrier(
        (to_owner(ask), sibling_lists, target, to_sibling(target))
    )
    picked = pick_tiles(asked, own, near_basis, space)
    order = permute_order(space)
    received = {}
    for at, j in enumerate(order):
        x = picked[j - 1]
        if at >= IN_FLIGHT:
            before = order[at - IN_FLIGHT]
            x, received[before] = lax.optimization_barrier((x, received[before]))
        received[j] = to_distance(x, j)
    received = [received[j] for j in range(1, space)]
    remote_blocks = pick_remote_blocks(listing, blocks, received[len(received) // 2])
    far_half, received, remote_blocks = lax.optimization_barrier((far_half, received, remote_blocks))
    own_half = [kept_half] + far_half
    other_half = [to_sibling(x) for x in own_half]
    own_sums = remote_sums(listing, remote_blocks, received, weights)
    far_sums = [to_chip(own_sums, j) for j in range(1, chips)]
    near_sums = [own_sums, to_sibling(own_sums)]
    partial, rounded, prolong = local_prolong(
        core, basis_tiles, own_half, other_half, near_sums, [listing, sibling_lists[0]]
    )
    partial, rounded, *far_sums = lax.optimization_barrier((partial, rounded, *far_sums))
    far_sums += [to_sibling(x) for x in far_sums]
    far_lists = lists[1:] + sibling_lists[1:]
    sent, finished = finish_prolong(partial, rounded, far_sums, far_lists, asked, space)

    received_prolong = to_owner(sent)
    keep, send, remote_blocks, own_tiles = local_coarse(
        code, target, listing, far_lists, blocks, prolong, finished, fields, targets, step
    )
    arrived = to_sibling(send)
    given = remote_coarse(listing, remote_blocks, own_tiles, received_prolong)
    sibling_given = to_sibling(given)
    total, *rest = share_sums(
        chip, keep, arrived, target, listing, given, sibling_target, sibling_lists[0], sibling_given, chips
    )
    for j, part in enumerate(rest, 1):
        total = total + to_chip(part, j).astype(F32)
    return total


def solution(mesh):
    return jax.shard_map(
        per_device,
        mesh=mesh,
        in_specs=(
            P("space", "col", None, None),
            P("space", None, None),
            P("space", None),
            P("space", "col"),
            P("space", "col"),
            P("space"),
            P("space"),
            P("space", "col"),
        ),
        out_specs=P(("space", "col"), None, None),
        check_vma=False,
    )
```
